32 devices in a mesh: groups: 2 (over x), dp: 16 (over z, y, core).
Axes of the slice: x: 2, y: 2, z: 4, core: 2. Of those that a mesh axis runs over, the one named last changes fastest.
Arguments:
- train_features: bfloat16 [4096, 4096], P(None, ('groups', 'dp')), parts along dimension 1, may hold values from -0.099609375 to 0.099609375
- query_gradients: bfloat16 [4096, 32768], P(None, ('groups', 'dp')), parts along dimension 1, may hold values from -6 to 6
- block_pairs: int32 [64, 2], P(('groups', 'dp')), parts along dimension 0, may hold values from 0 to 127, as said below
- basis_out: float32 [128, 64], P('groups'), parts along dimension 0, may hold values from -0.75 to 0.75
- basis_in: float32 [128, 64], P('groups'), parts along dimension 0, may hold values from -0.75 to 0.75
- eigen_out: float32 [128], P('groups'), parts along dimension 0, may hold values from 0.1 to 2
- eigen_in: float32 [128], P('groups'), parts along dimension 0, may hold values from 0.1 to 2
- damping: float32 [2], P('groups'), parts along dimension 0, may hold values from 0.2 to 1
Outputs:
- scores: float32 [64, 128, 128], P(('groups', 'dp')), parts along dimension 0
The draws below stay inside these ranges and needn't reach their ends.
There are 2 independent parts, one for each index of `groups`. The reference program is written for one: setup_inputs(seed, part) draws one part's arguments, and reference() takes and returns one part's arrays. A program takes and returns all parts, laid end to end along the dimension named above; each array names one. Nothing has to cross between parts.
Inputs may be any that keep to these rules, and one draw needn't show every extreme that they name: `block_pairs`: each row is a pair (training block t, query block u); block b means examples b * 128 to (b + 1) * 128 - 1. The first column is below 16 and every training block appears in it. Of the 8 query blocks of one device, exactly 4 appear in the second column on 2 of the devices and exactly one on each other device.
All inputs are finite; a program needn't handle non-finite values.
Results may differ from the reference program's by a relative error of at most 0.0029.
Values may be sent and summed in bfloat16 or wider, within the bound.
No kernel may reach another device: no remote copies, remote signals or barrier semaphores. Data moves between devices by JAX's collectives and lax.ppermute only.
A program may use at most 128 MiB of HBM per device.

```python
import math
import jax
import jax.numpy as jnp
from jax import lax

PROJ_OUT = 64
PROJ_IN = 64
BLOCK_ROWS = 128
NAMED_MOST = 4
TRAIN_BLOCKS = 1
QUERY_BLOCKS = 8
FEATURES = 4096
TRAIN_TOTAL = 2048
QUERY_TOTAL = 16384
PAIR_TOTAL = 32
N_DP = 16


def draw_block_pairs(key, part):
    key = jax.random.fold_in(key, 17)
    subkeys = jax.random.split(key, 6)
    devices = N_DP
    hot_count = devices // 8
    named_total = hot_count * NAMED_MOST + devices - hot_count
    hot_order = jax.random.permutation(subkeys[0], devices)
    counts = jnp.where(hot_order < hot_count, NAMED_MOST, 1)
    ranking = jax.random.randint(subkeys[1], (devices, QUERY_BLOCKS), 0, 1 << 20) * QUERY_BLOCKS
    ranking = ranking + jnp.arange(QUERY_BLOCKS, dtype=jnp.int32)[None, :]
    ranking = ranking.at[devices - 1, QUERY_BLOCKS - 1].set(-1)
    local_order = jnp.argsort(ranking, axis=1)[:, :NAMED_MOST]
    global_ids = jnp.arange(devices, dtype=jnp.int32)[:, None] * QUERY_BLOCKS + local_order
    usable = jnp.arange(NAMED_MOST, dtype=jnp.int32)[None, :] < counts[:, None]
    flat_ids = global_ids.reshape(-1)
    sort_keys = jnp.where(usable.reshape(-1), 0, 1) * (devices * NAMED_MOST) + jnp.arange(devices * NAMED_MOST, dtype=jnp.int32)
    leading = jnp.argsort(sort_keys)
    named_list = flat_ids[leading][:named_total]
    repeats = named_list[jax.random.randint(subkeys[2], (PAIR_TOTAL - named_total,), 0, named_total)]
    query_column = jax.random.permutation(subkeys[3], jnp.concatenate([named_list, repeats]))
    train_blocks_all = devices * TRAIN_BLOCKS
    train_repeats = jax.random.randint(subkeys[4], (PAIR_TOTAL - train_blocks_all,), 0, train_blocks_all)
    train_column = jax.random.permutation(subkeys[5], jnp.concatenate([jnp.arange(train_blocks_all, dtype=jnp.int32), train_repeats]))
    return jnp.stack([train_column, query_column], axis=1).astype(jnp.int32)


def block_scale(key, dims, pieces, least, largest):
    loudness, own = 1.0, jax.random.fold_in(key, 6)
    for position, shards_of in pieces:
        steps = jnp.exp(jax.random.uniform(jax.random.fold_in(own, position), (shards_of,), jnp.float32, least / len(pieces), largest / len(pieces)))
        loudness = loudness * jnp.repeat(steps, dims[position] // shards_of).reshape([-1 if axis == position else 1 for axis in range(len(dims))])
    return loudness


def centred(own_key, dims, spread, limit, cuts=(), held_as=jnp.bfloat16):
    factor_of = block_scale(own_key, dims, cuts, -0.22, 0.18) if cuts else 1.0
    result = jax.random.normal(own_key, dims, jnp.float32) * spread * factor_of
    return jnp.minimum(jnp.maximum(result, -limit), limit).astype(held_as)


def setup_inputs(seed: int = 0, part: int = 0) -> dict:
    splits = jax.random.split(jax.random.key(seed), 9)
    own_keys = jax.random.split(jax.random.fold_in(splits[8], part), 9)
    train_features = centred(own_keys[0], (FEATURES, TRAIN_TOTAL), 0.015625, 0.099609375, ((1, 16),))
    query_gradients = centred(own_keys[1], (FEATURES, QUERY_TOTAL), 1.0, 6.0, ((1, 16),))
    block_pairs = draw_block_pairs(jax.random.fold_in(jax.random.fold_in(splits[8], part), 71), part)
    basis_out = centred(own_keys[3], (PROJ_OUT, PROJ_OUT), PROJ_OUT ** -0.5, 0.75, (), jnp.float32)
    basis_in = centred(own_keys[4], (PROJ_IN, PROJ_IN), PROJ_IN ** -0.5, 0.75, (), jnp.float32)
    eigen_out = jnp.clip(jnp.exp(jax.random.uniform(own_keys[5], (PROJ_OUT,), jnp.float32, math.log(0.1), math.log(2.0))), 0.1, 2.0)
    eigen_in = jnp.clip(jnp.exp(jax.random.uniform(own_keys[6], (PROJ_IN,), jnp.float32, math.log(0.1), math.log(2.0))), 0.1, 2.0)
    damping = jnp.clip(jnp.exp(jax.random.uniform(own_keys[7], (1,), jnp.float32, math.log(0.2), math.log(1.0))), 0.2, 1.0)
    return {"train_features": train_features, "query_gradients": query_gradients, "block_pairs": block_pairs, "basis_out": basis_out, "basis_in": basis_in, "eigen_out": eigen_out, "eigen_in": eigen_in, "damping": damping}


def precondition(gradients, basis_out, basis_in, eigen_out, eigen_in, damping):
    highest = lax.Precision.HIGHEST
    rotated = jnp.einsum("bi,abq->iaq", basis_in, gradients, precision=highest)
    spectral = jnp.einsum("ao,iaq->oiq", basis_out, rotated, precision=highest)
    scaled = spectral / (eigen_out[:, None, None] * eigen_in[None, :, None] + damping[0])
    partway = jnp.einsum("bi,oiq->boq", basis_in, scaled, precision=highest)
    return jnp.einsum("ao,boq->abq", basis_out, partway, precision=highest)


def reference(train_features, query_gradients, block_pairs, basis_out, basis_in, eigen_out, eigen_in, damping):
    def score_pair(pair):
        train_start = (pair[0] * BLOCK_ROWS).astype(jnp.int32)
        query_start = (pair[1] * BLOCK_ROWS).astype(jnp.int32)
        train_block = lax.dynamic_slice_in_dim(train_features, train_start, BLOCK_ROWS, 1)
        query_block = lax.dynamic_slice_in_dim(query_gradients, query_start, BLOCK_ROWS, 1)
        gradients = query_block.astype(jnp.float32).reshape(PROJ_OUT, PROJ_IN, BLOCK_ROWS)
        conditioned = precondition(gradients, basis_out, basis_in, eigen_out, eigen_in, damping)
        conditioned = conditioned.reshape(PROJ_OUT * PROJ_IN, BLOCK_ROWS).astype(jnp.bfloat16)
        return jnp.dot(train_block.T, conditioned, preferred_element_type=jnp.float32)

    return lax.map(score_pair, block_pairs.astype(jnp.int32))
```

```python
import functools

import jax
import jax.numpy as jnp
from jax import lax
from jax.experimental import pallas as pl
from jax.experimental.pallas import tpu as pltpu
from jax.sharding import PartitionSpec as P

SIDE = 64
COLS = 128
NAMED_MOST = 4
EXTRA = NAMED_MOST - 1
GROUPED = 4
WIDE = GROUPED * SIDE
TILES = SIDE // GROUPED
VMEM_LIMIT = 40 * 1024 * 1024
f32, bf16 = jnp.float32, jnp.bfloat16


def split(x):
    high = x.astype(bf16)
    return high, (x - high.astype(f32)).astype(bf16)


def mm(a, b):
    return jnp.dot(a, b, preferred_element_type=f32)


def mm_nt(a, b):
    return lax.dot_general(a, b, (((1,), (1,)), ((), ())), preferred_element_type=f32)


def mm3(a, b):
    return mm(a[0], b[0]) + (mm(a[0], b[1]) + mm(a[1], b[0]))


def iota(shape, axis):
    return lax.broadcasted_iota(jnp.int32, shape, axis)


def chosen(cond):
    return jnp.where(cond, 1.0, 0.0).astype(bf16)


def precondition_kernel(train, basis_in, basis_out, inverse, out, y_high, y_low, z_high, z_low):
    tall, flat, square = (WIDE, SIDE), (SIDE, WIDE), (WIDE, WIDE)
    pick_i = chosen(iota(tall, 0) // GROUPED == iota(tall, 1))
    pick_i_t = chosen(iota(flat, 1) // GROUPED == iota(flat, 0))
    pick_low = chosen(iota(tall, 0) % SIDE == iota(tall, 1))
    pick_low_t = chosen(iota(flat, 1) % SIDE == iota(flat, 0))
    row_a = iota(tall, 0) // (GROUPED * GROUPED) * GROUPED + iota(tall, 0) % GROUPED
    pick_a = chosen(row_a == iota(tall, 1))
    col_a = iota(flat, 1) // (GROUPED * GROUPED) * GROUPED + iota(flat, 1) % GROUPED
    pick_a_t = chosen(col_a == iota(flat, 0))
    r, c = iota(square, 0), iota(square, 1)
    same_in = r % GROUPED == c // SIDE
    same_in_t = c % GROUPED == r // SIDE
    same_out = r // GROUPED % GROUPED == c // SIDE
    same_out_t = c // GROUPED % GROUPED == r // SIDE

    def masked(cond, x):
        return jnp.where(cond, x, 0.0).astype(bf16)

    in_parts, out_parts = split(basis_in[...]), split(basis_out[...])
    w_in = [masked(same_in, mm(mm_nt(pick_i, b).astype(bf16), pick_low_t)) for b in in_parts]
    w_in_t = [masked(same_in_t, mm(mm(pick_low, b).astype(bf16), pick_i_t)) for b in in_parts]
    w_out = [masked(same_out, mm(mm(pick_a, b).astype(bf16), pick_low_t)) for b in out_parts]
    w_out_t = [masked(same_out_t, mm(mm_nt(pick_low, b).astype(bf16), pick_a_t)) for b in out_parts]

    for A in range(0, TILES, 2):
        x = jnp.concatenate([train[pl.ds((A + k) * WIDE, WIDE), :] for k in range(2)], axis=1)
        high, low = split(mm(w_in[0], x) + mm(w_in[1], x))
        for k in range(2):
            y_high[A + k] = high[:, k * COLS : (k + 1) * COLS].reshape(TILES, -1, COLS)
            y_low[A + k] = low[:, k * COLS : (k + 1) * COLS].reshape(TILES, -1, COLS)
    for g in range(0, TILES, 2):
        y = [jnp.concatenate([ref[:, g + k].reshape(WIDE, COLS) for k in range(2)], axis=1) for ref in (y_high, y_low)]
        s = mm3(w_out_t, y)
        factor = [jnp.broadcast_to(inverse[:, g + k : g + k + 1], (WIDE, COLS)) for k in range(2)]
        high, low = split(mm3(w_out, split(s * jnp.concatenate(factor, axis=1))))
        for k in range(2):
            z_high[:, g + k] = high[:, k * COLS : (k + 1) * COLS].reshape(TILES, -1, COLS)
            z_low[:, g + k] = low[:, k * COLS : (k + 1) * COLS].reshape(TILES, -1, COLS)
    share = out.shape[2]
    for A in range(0, TILES, 2):
        z = [jnp.concatenate([ref[A + k].reshape(WIDE, COLS) for k in range(2)], axis=1) for ref in (z_high, z_low)]
        result = mm3(w_in_t, z)
        for k in range(2):
            turned = result[:, k * COLS : (k + 1) * COLS].T.astype(bf16)
            for part in range(WIDE // share):
                out[(A + k) * (WIDE // share) + part] = turned[:, part * share : (part + 1) * share]


def precondition(train, basis_in, basis_out, inverse, chunks):
    features = train.shape[0]
    tiled = pltpu.VMEM((TILES, TILES, WIDE // TILES, COLS), bf16)
    return pl.pallas_call(
        precondition_kernel,
        out_shape=jax.ShapeDtypeStruct((chunks, COLS, features // chunks), bf16),
        in_specs=[pl.BlockSpec(memory_space=pltpu.VMEM)] * 4,
        out_specs=pl.BlockSpec(memory_space=pltpu.VMEM),
        scratch_shapes=[tiled] * 4,
        compiler_params=pltpu.CompilerParams(vmem_limit_bytes=VMEM_LIMIT),
        cost_estimate=pl.CostEstimate(flops=3_000_000_000, bytes_accessed=4 * features * COLS, transcendentals=0),
        name="precondition",
    )(train, basis_in, basis_out, inverse)


def score_kernel(per_device, rows, train, first, extra, keep, send):
    core = rows[2, 0]
    devices = first.shape[0]

    def tile(pair):
        slot = rows[1, pair]
        a = first[jnp.minimum(slot, devices - 1)]
        b = extra[jnp.maximum(slot - devices, 0)]
        q = jnp.where(slot < devices, a.astype(f32), b.astype(f32)).astype(bf16)
        return mm(train[rows[0, pair]], q)

    def step(h, carry):
        base = h // per_device * (2 * per_device) + h % per_device
        keep[h] = tile(base + core * per_device)
        send[h] = tile(base + (1 - core) * per_device)
        return carry

    lax.fori_loop(0, keep.shape[0], step, 0, unroll=4)


def partial_scores(rows, per_device, train, first, extra):
    half = rows.shape[1] // 2
    tiles = jax.ShapeDtypeStruct((half, COLS, COLS), f32)
    whole = pl.BlockSpec(memory_space=pltpu.VMEM)
    return pl.pallas_call(
        functools.partial(score_kernel, per_device),
        out_shape=(tiles, tiles),
        in_specs=[pl.BlockSpec(memory_space=pltpu.SMEM), whole, whole, whole],
        out_specs=(whole, whole),
        compiler_params=pltpu.CompilerParams(vmem_limit_bytes=VMEM_LIMIT),
        name="partial_scores",
    )(rows, train, first, extra)


def body(devices, train_features, query_gradients, block_pairs, basis_out, basis_in, eigen_out, eigen_in, damping):
    bits = devices.bit_length() - 1
    me = lax.axis_index("dp")
    mine = [(me >> b) & 1 for b in range(bits)]
    features, local_columns = query_gradients.shape
    local_blocks = local_columns // COLS
    per_device = block_pairs.shape[0]
    share = features // devices
    hot_total = devices // 8

    def across(x, b):
        return lax.ppermute(x, "dp", [(d, d ^ (1 << b)) for d in range(devices)])

    pairs = block_pairs
    for b in range(bits):
        other = across(pairs, b)
        pairs = jnp.where(mine[b] == 0, jnp.concatenate([pairs, other]), jnp.concatenate([other, pairs]))

    inverse = 1.0 / (eigen_out[None, :, None] * eigen_in.reshape(TILES, GROUPED).T[:, None, :] + damping[0])
    conditioned = precondition(train_features, basis_in, basis_out, inverse.reshape(WIDE, TILES), devices)
    train_share = lax.all_to_all(conditioned, "dp", split_axis=0, concat_axis=0, tiled=True)

    blocks = jnp.arange(devices * local_blocks, dtype=jnp.int32)
    named = jnp.any(pairs[:, 1:2] == blocks[None, :], axis=0).reshape(devices, local_blocks)
    ahead = jnp.arange(local_blocks)[:, None] < jnp.arange(local_blocks)[None, :]
    order = jnp.sum(jnp.where(named[:, :, None] & ahead[None], 1, 0), axis=1)
    hot = jnp.sum(named.astype(jnp.int32), axis=1) > 1
    earlier = jnp.arange(devices)[:, None] < jnp.arange(devices)[None, :]
    hot_order = jnp.sum(jnp.where(hot[:, None] & earlier, 1, 0), axis=0)
    slot = jnp.where(
        order == 0, jnp.arange(devices)[:, None], devices + EXTRA * hot_order[:, None] + order - 1
    ).reshape(-1)
    pair_slot = jnp.sum(jnp.where(pairs[:, 1:2] == blocks[None, :], slot[None, :], 0), axis=1)
    rows = jnp.stack([pairs[:, 0], pair_slot, jnp.broadcast_to(mine[0], pair_slot.shape)]).astype(jnp.int32)

    own_named = lax.dynamic_index_in_dim(named, me, 0, False)
    own_order = lax.dynamic_index_in_dim(order, me, 0, False)
    local_ids = jnp.arange(local_blocks, dtype=jnp.int32)

    def named_block(k):
        which = jnp.sum(jnp.where(own_named & (own_order == k), local_ids, 0))
        return lax.dynamic_slice_in_dim(query_gradients, which * COLS, COLS, 1)

    own = jnp.stack([named_block(k) for k in range(1, NAMED_MOST)])
    own = own.reshape((EXTRA,) + (2,) * bits + (share, COLS))

    def halves(x, b, left):
        axis = 1 + [k for k in sorted(left, reverse=True)].index(b)
        keep = lax.dynamic_index_in_dim(x, mine[b], axis, False)
        return keep, lax.dynamic_index_in_dim(x, 1 - mine[b], axis, False)

    keep, send = halves(own, 0, list(range(bits)))
    other = across(send, 0)
    chains = []
    for rank in range(hot_total):
        is_rank = hot & (hot_order == rank)
        from_me = is_rank[me]
        from_other = is_rank[me ^ 1]
        x = jnp.where(from_me, keep, jnp.where(from_other, other, jnp.zeros_like(other)))
        rest = list(range(1, bits))
        turn = rank % 2
        chains.append([x, rest[turn : turn + 1] + rest[:turn] + rest[turn + 1 :], rest])

    first_share = lax.all_to_all(
        named_block(0).reshape(devices, share, COLS), "dp", split_axis=0, concat_axis=0, tiled=True
    )

    for _ in range(1, bits):
        for chain in chains:
            x, todo, left = chain
            b = todo.pop(0)
            keep, send = halves(x, b, left)
            left.remove(b)
            chain[0] = keep + across(send, b)
    extra_share = jnp.concatenate([chain[0] for chain in chains], axis=0)

    keep, send = partial_scores(rows, per_device, train_share, first_share, extra_share)
    tiles = keep + across(send, 0)
    tiles = tiles.reshape((2,) * (bits - 1) + (per_device, COLS, COLS))
    for b in range(1, bits):
        axis = bits - 1 - b
        keep = lax.dynamic_index_in_dim(tiles, mine[b], axis, False)
        send = lax.dynamic_index_in_dim(tiles, 1 - mine[b], axis, False)
        if b == 1:
            tiles = keep + across(send.astype(bf16), b).astype(f32)
        else:
            tiles = keep + across(send, b)
    return tiles


def solution(mesh):
    placed = (
        P(None, ("groups", "dp")),
        P(None, ("groups", "dp")),
        P(("groups", "dp"), None),
        P("groups", None),
        P("groups", None),
        P("groups"),
        P("groups"),
        P("groups"),
    )
    return jax.shard_map(
        functools.partial(body, mesh.shape["dp"]),
        mesh=mesh,
        in_specs=placed,
        out_specs=P(("groups", "dp"), None, None),
        check_vma=False,
    )
```

```python
import functools

import jax
import jax.numpy as jnp
from jax import lax
from jax.experimental import pallas as pl
from jax.experimental.pallas import tpu as pltpu
from jax.sharding import PartitionSpec as P

SIDE = 64
COLS = 128
NAMED_MOST = 4
EXTRA = NAMED_MOST - 1
GROUPED = 4
WIDE = GROUPED * SIDE
TILES = SIDE // GROUPED
VMEM_LIMIT = 40 * 1024 * 1024
FULL_VMEM = 60 * 1024 * 1024
f32, bf16 = jnp.float32, jnp.bfloat16


def split(x):
    high = x.astype(bf16)
    return high, (x - high.astype(f32)).astype(bf16)


def mm(a, b):
    return jnp.dot(a, b, preferred_element_type=f32)


def mm_nt(a, b):
    return lax.dot_general(a, b, (((1,), (1,)), ((), ())), preferred_element_type=f32)


def mm3(a, b):
    return mm(a[0], b[0]) + (mm(a[0], b[1]) + mm(a[1], b[0]))


def iota(shape, axis):
    return lax.broadcasted_iota(jnp.int32, shape, axis)


def chosen(cond):
    return jnp.where(cond, 1.0, 0.0).astype(bf16)


def precondition_kernel(train, basis_in, basis_out, inverse, out, y_high, y_low, z_high, z_low):
    tall, flat, square = (WIDE, SIDE), (SIDE, WIDE), (WIDE, WIDE)
    pick_i = chosen(iota(tall, 0) // GROUPED == iota(tall, 1))
    pick_i_t = chosen(iota(flat, 1) // GROUPED == iota(flat, 0))
    pick_low = chosen(iota(tall, 0) % SIDE == iota(tall, 1))
    pick_low_t = chosen(iota(flat, 1) % SIDE == iota(flat, 0))
    row_a = iota(tall, 0) // (GROUPED * GROUPED) * GROUPED + iota(tall, 0) % GROUPED
    pick_a = chosen(row_a == iota(tall, 1))
    col_a = iota(flat, 1) // (GROUPED * GROUPED) * GROUPED + iota(flat, 1) % GROUPED
    pick_a_t = chosen(col_a == iota(flat, 0))
    r, c = iota(square, 0), iota(square, 1)
    same_in = r % GROUPED == c // SIDE
    same_in_t = c % GROUPED == r // SIDE
    same_out = r // GROUPED % GROUPED == c // SIDE
    same_out_t = c // GROUPED % GROUPED == r // SIDE

    def masked(cond, x):
        return jnp.where(cond, x, 0.0).astype(bf16)

    in_parts, out_parts = split(basis_in[...]), split(basis_out[...])
    w_in = [masked(same_in, mm(mm_nt(pick_i, b).astype(bf16), pick_low_t)) for b in in_parts]
    w_in_t = [masked(same_in_t, mm(mm(pick_low, b).astype(bf16), pick_i_t)) for b in in_parts]
    w_out = [masked(same_out, mm(mm(pick_a, b).astype(bf16), pick_low_t)) for b in out_parts]
    w_out_t = [masked(same_out_t, mm(mm_nt(pick_low, b).astype(bf16), pick_a_t)) for b in out_parts]

    for A in range(0, TILES, 2):
        x = jnp.concatenate([train[pl.ds((A + k) * WIDE, WIDE), :] for k in range(2)], axis=1)
        high, low = split(mm(w_in[0], x) + mm(w_in[1], x))
        for k in range(2):
            y_high[A + k] = high[:, k * COLS : (k + 1) * COLS].reshape(TILES, -1, COLS)
            y_low[A + k] = low[:, k * COLS : (k + 1) * COLS].reshape(TILES, -1, COLS)
    for g in range(0, TILES, 2):
        y = [jnp.concatenate([ref[:, g + k].reshape(WIDE, COLS) for k in range(2)], axis=1) for ref in (y_high, y_low)]
        s = mm3(w_out_t, y)
        factor = [jnp.broadcast_to(inverse[:, g + k : g + k + 1], (WIDE, COLS)) for k in range(2)]
        high, low = split(mm3(w_out, split(s * jnp.concatenate(factor, axis=1))))
        for k in range(2):
            z_high[:, g + k] = high[:, k * COLS : (k + 1) * COLS].reshape(TILES, -1, COLS)
            z_low[:, g + k] = low[:, k * COLS : (k + 1) * COLS].reshape(TILES, -1, COLS)
    share = out.shape[2]
    for A in range(0, TILES, 2):
        z = [jnp.concatenate([ref[A + k].reshape(WIDE, COLS) for k in range(2)], axis=1) for ref in (z_high, z_low)]
        result = mm3(w_in_t, z)
        for k in range(2):
            turned = result[:, k * COLS : (k + 1) * COLS].T.astype(bf16)
            for part in range(WIDE // share):
                out[(A + k) * (WIDE // share) + part] = turned[:, part * share : (part + 1) * share]


def precondition(train, basis_in, basis_out, inverse, chunks):
    features = train.shape[0]
    tiled = pltpu.VMEM((TILES, TILES, WIDE // TILES, COLS), bf16)
    return pl.pallas_call(
        precondition_kernel,
        out_shape=jax.ShapeDtypeStruct((chunks, COLS, features // chunks), bf16),
        in_specs=[pl.BlockSpec(memory_space=pltpu.VMEM)] * 4,
        out_specs=pl.BlockSpec(memory_space=pltpu.VMEM),
        scratch_shapes=[tiled] * 4,
        compiler_params=pltpu.CompilerParams(vmem_limit_bytes=VMEM_LIMIT),
        cost_estimate=pl.CostEstimate(flops=3_000_000_000, bytes_accessed=4 * features * COLS, transcendentals=0),
        name="precondition",
    )(train, basis_in, basis_out, inverse)


def score_kernel(per_device, rows, train, first, extra, keep, send):
    core = rows[2, 0]
    devices = first.shape[0]

    def tile(pair):
        slot = rows[1, pair]
        a = first[jnp.minimum(slot, devices - 1)]
        b = extra[jnp.maximum(slot - devices, 0)]
        q = jnp.where(slot < devices, a.astype(f32), b.astype(f32)).astype(bf16)
        return mm(train[rows[0, pair]], q)

    def step(h, carry):
        base = h // per_device * (2 * per_device) + h % per_device
        keep[h] = tile(base + core * per_device)
        send[h] = tile(base + (1 - core) * per_device)
        return carry

    lax.fori_loop(0, keep.shape[0], step, 0, unroll=4)


def partial_scores(rows, per_device, train, first, extra):
    half = rows.shape[1] // 2
    tiles = jax.ShapeDtypeStruct((half, COLS, COLS), f32)
    whole = pl.BlockSpec(memory_space=pltpu.VMEM)
    return pl.pallas_call(
        functools.partial(score_kernel, per_device),
        out_shape=(tiles, tiles),
        in_specs=[pl.BlockSpec(memory_space=pltpu.SMEM), whole, whole, whole],
        out_specs=(whole, whole),
        compiler_params=pltpu.CompilerParams(vmem_limit_bytes=VMEM_LIMIT),
        name="partial_scores",
    )(rows, train, first, extra)


def plan_kernel(
    me_ref, pairs, query, rows, hots, first, keep, send, masks, ranks, own, first_sem, keep_sem, send_sem
):
    me = me_ref[0]
    devices, total = masks.shape[0], pairs.shape[0]
    local_blocks = query.shape[3] // COLS
    level = local_blocks.bit_length() - 1

    @pl.loop(0, devices, unroll=8)
    def _(d):
        masks[d] = 0

    @pl.loop(0, total, unroll=8)
    def _(p):
        block = pairs[p, 1]
        d = lax.shift_right_logical(block, level)
        masks[d] = masks[d] | lax.shift_left(1, block & (local_blocks - 1))

    count = jnp.int32(0)
    mask = masks[me]
    for k in range(local_blocks):
        bit = lax.shift_right_logical(mask, k) & 1

        @pl.when(bit == 1)
        def _():
            own[jnp.minimum(count, EXTRA)] = k

        count = count + bit
    is_hot = count > 1

    def cut(k, source, target, sem):
        start = pl.multiple_of(own[k] * COLS, COLS)
        return pltpu.make_async_copy(source.at[..., pl.ds(start, COLS)], target, sem)

    core = me & 1
    first_copy = cut(0, query, first, first_sem)
    first_copy.start()

    def extra_copies(k):
        return (
            cut(k + 1, query.at[:, core], keep.at[k], keep_sem.at[k]),
            cut(k + 1, query.at[:, 1 - core], send.at[k], send_sem.at[k]),
        )

    @pl.when(is_hot)
    def _():
        for k in range(EXTRA):
            for copy in extra_copies(k):
                copy.start()

    def rank_step(d, rank):
        mask = masks[d]
        hot = (mask & (mask - 1)) != 0

        ranks[d] = rank

        @pl.when(hot)
        def _():
            hots[jnp.minimum(rank, hots.shape[0] - 1)] = d

        return rank + jnp.where(hot, 1, 0)

    lax.fori_loop(0, devices, rank_step, jnp.int32(0), unroll=4)

    @pl.loop(0, total, unroll=4)
    def _(p):
        block = pairs[p, 1]
        d = lax.shift_right_logical(block, level)
        before = masks[d] & (lax.shift_left(1, block & (local_blocks - 1)) - 1)
        order = before & 1
        for k in range(1, local_blocks):
            order = order + (lax.shift_right_logical(before, k) & 1)
        rows[0, p] = pairs[p, 0]
        rows[1, p] = jnp.where(order == 0, d, devices + EXTRA * ranks[d] + order - 1)

    first_copy.wait()

    @pl.when(is_hot)
    def _():
        for k in range(EXTRA):
            for copy in extra_copies(k):
                copy.wait()


def plan(me, pairs, query, devices, share, hot_total):
    smem, hbm = pl.BlockSpec(memory_space=pltpu.SMEM), pl.BlockSpec(memory_space=pl.ANY)
    vmem = pl.BlockSpec(memory_space=pltpu.VMEM)
    half = devices // 2
    extra = jax.ShapeDtypeStruct((EXTRA, half, share, COLS), bf16)
    return pl.pallas_call(
        plan_kernel,
        out_shape=(
            jax.ShapeDtypeStruct((2, pairs.shape[0]), jnp.int32),
            jax.ShapeDtypeStruct((hot_total,), jnp.int32),
            jax.ShapeDtypeStruct((half, 2, share, COLS), bf16),
            extra,
            extra,
        ),
        in_specs=[smem, smem, hbm],
        out_specs=(smem, smem, vmem, vmem, vmem),
        scratch_shapes=[
            pltpu.SMEM((devices,), jnp.int32),
            pltpu.SMEM((devices,), jnp.int32),
            pltpu.SMEM((NAMED_MOST,), jnp.int32),
            pltpu.SemaphoreType.DMA,
            pltpu.SemaphoreType.DMA((EXTRA,)),
            pltpu.SemaphoreType.DMA((EXTRA,)),
        ],
        compiler_params=pltpu.CompilerParams(vmem_limit_bytes=FULL_VMEM),
        name="plan",
    )(me.reshape(1), pairs, query.reshape(half, 2, share, -1))


def body(devices, train_features, query_gradients, block_pairs, basis_out, basis_in, eigen_out, eigen_in, damping):
    bits = devices.bit_length() - 1
    me = lax.axis_index("dp").astype(jnp.int32)
    mine = [(me >> b) & 1 for b in range(bits)]
    per_device = block_pairs.shape[0]
    share = query_gradients.shape[0] // devices
    hot_total = devices // 8

    def across(x, b):
        return lax.ppermute(x, "dp", [(d, d ^ (1 << b)) for d in range(devices)])

    def to_all(x):
        return lax.all_to_all(x, "dp", split_axis=0, concat_axis=0, tiled=True)

    pairs = block_pairs
    for b in range(bits):
        other = across(pairs, b)
        pairs = jnp.where(mine[b] == 0, jnp.concatenate([pairs, other]), jnp.concatenate([other, pairs]))

    rows, hots, first, keep, send = plan(me, pairs, query_gradients, devices, share, hot_total)
    first_share = to_all(first.reshape(devices, share, COLS))
    def halves(x, b, left):
        axis = 1 + sorted(left, reverse=True).index(b)
        left.remove(b)
        keep = lax.dynamic_index_in_dim(x, mine[b], axis, False)
        return keep, lax.dynamic_index_in_dim(x, 1 - mine[b], axis, False)

    def arrived(hot, b, keep, other):
        return jnp.where(((me ^ hot) >> b) & 1 == 1, other, keep)

    inverse = 1.0 / (eigen_out[None, :, None] * eigen_in.reshape(TILES, GROUPED).T[:, None, :] + damping[0])
    other = across(send, 0)
    keep, other = (x.reshape((EXTRA,) + (2,) * (bits - 1) + (share, COLS)) for x in (keep, other))
    chains = []
    for rank in range(hot_total):
        rest = list(range(1, bits))
        turn = rank % 2
        steps = rest[turn : turn + 1] + rest[:turn] + rest[turn + 1 :]
        chains.append([arrived(hots[rank], 0, keep, other), steps, rest])

    for k in range(bits - 1):
        parts = [halves(x, steps[k], left) for x, steps, left in chains]
        sends = [part[1] for part in parts]
        if k == 0:
            *sends, inverse = lax.optimization_barrier((*sends, inverse))
            conditioned = precondition(train_features, basis_in, basis_out, inverse.reshape(WIDE, TILES), devices)
            conditioned, first_share = lax.optimization_barrier((conditioned, first_share))
            train_share = to_all(conditioned)
        if k == bits - 2:
            *sends, train_share = lax.optimization_barrier((*sends, train_share))
        others = [across(send, chain[1][k]) for send, chain in zip(sends, chains)]
        others = lax.optimization_barrier(others)
        for rank, chain in enumerate(chains):
            chain[0] = arrived(hots[rank], chain[1][k], parts[rank][0], others[rank])
    extra_share = jnp.concatenate([chain[0] for chain in chains], axis=0)

    rows = jnp.concatenate([rows, jnp.broadcast_to(mine[0], (1, rows.shape[1]))])
    keep, send = partial_scores(rows, per_device, train_share, first_share, extra_share)
    tiles = keep + across(send, 0)
    tiles = tiles.reshape((2,) * (bits - 1) + (per_device, COLS, COLS))
    for b in range(1, bits):
        axis = bits - 1 - b
        keep = lax.dynamic_index_in_dim(tiles, mine[b], axis, False)
        send = lax.dynamic_index_in_dim(tiles, 1 - mine[b], axis, False)
        if b == 1:
            tiles = keep + across(send.astype(bf16), b).astype(f32)
        else:
            tiles = keep + across(send, b)
    return tiles


def solution(mesh):
    placed = (
        P(None, ("groups", "dp")),
        P(None, ("groups", "dp")),
        P(("groups", "dp"), None),
        P("groups", None),
        P("groups", None),
        P("groups"),
        P("groups"),
        P("groups"),
    )
    return jax.shard_map(
        functools.partial(body, mesh.shape["dp"]),
        mesh=mesh,
        in_specs=placed,
        out_specs=P(("groups", "dp"), None, None),
        check_vma=False,
    )
```

```python
import functools

import jax
import jax.numpy as jnp
from jax import lax
from jax.experimental import pallas as pl
from jax.experimental.pallas import tpu as pltpu
from jax.sharding import PartitionSpec as P

SIDE = 64
COLS = 128
NAMED_MOST = 4
EXTRA = NAMED_MOST - 1
GROUPED = 4
WIDE = GROUPED * SIDE
TILES = SIDE // GROUPED
VMEM_LIMIT = 40 * 1024 * 1024
FULL_VMEM = 60 * 1024 * 1024
f32, bf16 = jnp.float32, jnp.bfloat16


def split(x):
    high = x.astype(bf16)
    return high, (x - high.astype(f32)).astype(bf16)


def mm(a, b):
    return jnp.dot(a, b, preferred_element_type=f32)


def mm_nt(a, b):
    return lax.dot_general(a, b, (((1,), (1,)), ((), ())), preferred_element_type=f32)


def mm3(a, b):
    return mm(a[0], b[0]) + (mm(a[0], b[1]) + mm(a[1], b[0]))


def iota(shape, axis):
    return lax.broadcasted_iota(jnp.int32, shape, axis)


def chosen(cond):
    return jnp.where(cond, 1.0, 0.0).astype(bf16)


def precondition_kernel(train, basis_in, basis_out, inverse, out, y_high, y_low, z_high, z_low):
    tall, flat, square = (WIDE, SIDE), (SIDE, WIDE), (WIDE, WIDE)
    pick_i = chosen(iota(tall, 0) // GROUPED == iota(tall, 1))
    pick_i_t = chosen(iota(flat, 1) // GROUPED == iota(flat, 0))
    pick_low = chosen(iota(tall, 0) % SIDE == iota(tall, 1))
    pick_low_t = chosen(iota(flat, 1) % SIDE == iota(flat, 0))
    row_a = iota(tall, 0) // (GROUPED * GROUPED) * GROUPED + iota(tall, 0) % GROUPED
    pick_a = chosen(row_a == iota(tall, 1))
    col_a = iota(flat, 1) // (GROUPED * GROUPED) * GROUPED + iota(flat, 1) % GROUPED
    pick_a_t = chosen(col_a == iota(flat, 0))
    r, c = iota(square, 0), iota(square, 1)
    same_in = r % GROUPED == c // SIDE
    same_in_t = c % GROUPED == r // SIDE
    same_out = r // GROUPED % GROUPED == c // SIDE
    same_out_t = c // GROUPED % GROUPED == r // SIDE

    def masked(cond, x):
        return jnp.where(cond, x, 0.0).astype(bf16)

    in_parts, out_parts = split(basis_in[...]), split(basis_out[...])
    w_in = [masked(same_in, mm(mm_nt(pick_i, b).astype(bf16), pick_low_t)) for b in in_parts]
    w_in_t = [masked(same_in_t, mm(mm(pick_low, b).astype(bf16), pick_i_t)) for b in in_parts]
    w_out = [masked(same_out, mm(mm(pick_a, b).astype(bf16), pick_low_t)) for b in out_parts]
    w_out_t = [masked(same_out_t, mm(mm_nt(pick_low, b).astype(bf16), pick_a_t)) for b in out_parts]

    for A in range(0, TILES, 2):
        x = jnp.concatenate([train[pl.ds((A + k) * WIDE, WIDE), :] for k in range(2)], axis=1)
        high, low = split(mm(w_in[0], x) + mm(w_in[1], x))
        for k in range(2):
            y_high[A + k] = high[:, k * COLS : (k + 1) * COLS].reshape(TILES, -1, COLS)
            y_low[A + k] = low[:, k * COLS : (k + 1) * COLS].reshape(TILES, -1, COLS)
    for g in range(0, TILES, 2):
        y = [jnp.concatenate([ref[:, g + k].reshape(WIDE, COLS) for k in range(2)], axis=1) for ref in (y_high, y_low)]
        s = mm3(w_out_t, y)
        factor = [jnp.broadcast_to(inverse[:, g + k : g + k + 1], (WIDE, COLS)) for k in range(2)]
        high, low = split(mm3(w_out, split(s * jnp.concatenate(factor, axis=1))))
        for k in range(2):
            z_high[:, g + k] = high[:, k * COLS : (k + 1) * COLS].reshape(TILES, -1, COLS)
            z_low[:, g + k] = low[:, k * COLS : (k + 1) * COLS].reshape(TILES, -1, COLS)
    share = out.shape[2]
    for A in range(0, TILES, 2):
        z = [jnp.concatenate([ref[A + k].reshape(WIDE, COLS) for k in range(2)], axis=1) for ref in (z_high, z_low)]
        result = mm3(w_in_t, z)
        for k in range(2):
            turned = result[:, k * COLS : (k + 1) * COLS].T.astype(bf16)
            for part in range(WIDE // share):
                out[(A + k) * (WIDE // share) + part] = turned[:, part * share : (part + 1) * share]


def precondition(train, basis_in, basis_out, inverse, chunks):
    features = train.shape[0]
    tiled = pltpu.VMEM((TILES, TILES, WIDE // TILES, COLS), bf16)
    return pl.pallas_call(
        precondition_kernel,
        out_shape=jax.ShapeDtypeStruct((chunks, COLS, features // chunks), bf16),
        in_specs=[pl.BlockSpec(memory_space=pltpu.VMEM)] * 4,
        out_specs=pl.BlockSpec(memory_space=pltpu.VMEM),
        scratch_shapes=[tiled] * 4,
        compiler_params=pltpu.CompilerParams(vmem_limit_bytes=VMEM_LIMIT),
        cost_estimate=pl.CostEstimate(flops=3_000_000_000, bytes_accessed=4 * features * COLS, transcendentals=0),
        name="precondition",
    )(train, basis_in, basis_out, inverse)


def score_kernel(per_device, rows, train, first, extra, keep, send):
    core = rows[2, 0]
    devices = first.shape[0]

    def tile(pair):
        slot = rows[1, pair]
        a = first[jnp.minimum(slot, devices - 1)]
        b = extra[jnp.maximum(slot - devices, 0)]
        q = jnp.where(slot < devices, a.astype(f32), b.astype(f32)).astype(bf16)
        return mm(train[rows[0, pair]], q)

    def step(h, carry):
        base = h // per_device * (2 * per_device) + h % per_device
        keep[h] = tile(base + core * per_device)
        send[h] = tile(base + (1 - core) * per_device)
        return carry

    lax.fori_loop(0, keep.shape[0], step, 0, unroll=4)


def partial_scores(rows, per_device, train, first, extra):
    half = rows.shape[1] // 2
    tiles = jax.ShapeDtypeStruct((half, COLS, COLS), f32)
    whole = pl.BlockSpec(memory_space=pltpu.VMEM)
    return pl.pallas_call(
        functools.partial(score_kernel, per_device),
        out_shape=(tiles, tiles),
        in_specs=[pl.BlockSpec(memory_space=pltpu.SMEM), whole, whole, whole],
        out_specs=(whole, whole),
        compiler_params=pltpu.CompilerParams(vmem_limit_bytes=VMEM_LIMIT),
        name="partial_scores",
    )(rows, train, first, extra)


def plan_kernel(
    me_ref, pairs, query, rows, hots, first, keep, send, masks, ranks, own, first_sem, keep_sem, send_sem
):
    me = me_ref[0]
    devices, total = masks.shape[0], pairs.shape[0]
    local_blocks = query.shape[3] // COLS
    level = local_blocks.bit_length() - 1

    @pl.loop(0, devices, unroll=8)
    def _(d):
        masks[d] = 0

    @pl.loop(0, total, unroll=8)
    def _(p):
        block = pairs[p, 1]
        d = lax.shift_right_logical(block, level)
        masks[d] = masks[d] | lax.shift_left(1, block & (local_blocks - 1))

    count = jnp.int32(0)
    mask = masks[me]
    for k in range(local_blocks):
        bit = lax.shift_right_logical(mask, k) & 1

        @pl.when(bit == 1)
        def _():
            own[jnp.minimum(count, EXTRA)] = k

        count = count + bit
    is_hot = count > 1

    def cut(k, source, target, sem):
        start = pl.multiple_of(own[k] * COLS, COLS)
        return pltpu.make_async_copy(source.at[..., pl.ds(start, COLS)], target, sem)

    core = me & 1
    first_copy = cut(0, query, first, first_sem)
    first_copy.start()

    def extra_copies(k):
        return (
            cut(k + 1, query.at[:, core], keep.at[k], keep_sem.at[k]),
            cut(k + 1, query.at[:, 1 - core], send.at[k], send_sem.at[k]),
        )

    @pl.when(is_hot)
    def _():
        for k in range(EXTRA):
            for copy in extra_copies(k):
                copy.start()

    def rank_step(d, rank):
        mask = masks[d]
        hot = (mask & (mask - 1)) != 0

        ranks[d] = rank

        @pl.when(hot)
        def _():
            hots[jnp.minimum(rank, hots.shape[0] - 1)] = d

        return rank + jnp.where(hot, 1, 0)

    lax.fori_loop(0, devices, rank_step, jnp.int32(0), unroll=4)

    @pl.loop(0, total, unroll=4)
    def _(p):
        block = pairs[p, 1]
        d = lax.shift_right_logical(block, level)
        before = masks[d] & (lax.shift_left(1, block & (local_blocks - 1)) - 1)
        order = before & 1
        for k in range(1, local_blocks):
            order = order + (lax.shift_right_logical(before, k) & 1)
        rows[0, p] = pairs[p, 0]
        rows[1, p] = jnp.where(order == 0, d, devices + EXTRA * ranks[d] + order - 1)

    first_copy.wait()

    @pl.when(is_hot)
    def _():
        for k in range(EXTRA):
            for copy in extra_copies(k):
                copy.wait()


def plan(me, pairs, query, devices, share, hot_total):
    smem, hbm = pl.BlockSpec(memory_space=pltpu.SMEM), pl.BlockSpec(memory_space=pl.ANY)
    vmem = pl.BlockSpec(memory_space=pltpu.VMEM)
    half = devices // 2
    extra = jax.ShapeDtypeStruct((EXTRA, half, share, COLS), bf16)
    return pl.pallas_call(
        plan_kernel,
        out_shape=(
            jax.ShapeDtypeStruct((2, pairs.shape[0]), jnp.int32),
            jax.ShapeDtypeStruct((hot_total,), jnp.int32),
            jax.ShapeDtypeStruct((half, 2, share, COLS), bf16),
            extra,
            extra,
        ),
        in_specs=[smem, smem, hbm],
        out_specs=(smem, smem, vmem, vmem, vmem),
        scratch_shapes=[
            pltpu.SMEM((devices,), jnp.int32),
            pltpu.SMEM((devices,), jnp.int32),
            pltpu.SMEM((NAMED_MOST,), jnp.int32),
            pltpu.SemaphoreType.DMA,
            pltpu.SemaphoreType.DMA((EXTRA,)),
            pltpu.SemaphoreType.DMA((EXTRA,)),
        ],
        compiler_params=pltpu.CompilerParams(vmem_limit_bytes=FULL_VMEM),
        name="plan",
    )(me.reshape(1), pairs, query.reshape(half, 2, share, -1))


def body(devices, train_features, query_gradients, block_pairs, basis_out, basis_in, eigen_out, eigen_in, damping):
    bits = devices.bit_length() - 1
    me = lax.axis_index("dp").astype(jnp.int32)
    mine = [(me >> b) & 1 for b in range(bits)]
    per_device = block_pairs.shape[0]
    share = query_gradients.shape[0] // devices
    hot_total = devices // 8

    def across(x, b):
        return lax.ppermute(x, "dp", [(d, d ^ (1 << b)) for d in range(devices)])

    def to_all(x):
        return lax.all_to_all(x, "dp", split_axis=0, concat_axis=0, tiled=True)

    pairs = block_pairs
    for b in range(bits):
        other = across(pairs, b)
        pairs = jnp.where(mine[b] == 0, jnp.concatenate([pairs, other]), jnp.concatenate([other, pairs]))

    rows, hots, first, keep, send = plan(me, pairs, query_gradients, devices, share, hot_total)
    first_share = to_all(first.reshape(devices, share, COLS))
    def halves(x, b, left):
        axis = 1 + sorted(left, reverse=True).index(b)
        left.remove(b)
        keep = lax.dynamic_index_in_dim(x, mine[b], axis, False)
        return keep, lax.dynamic_index_in_dim(x, 1 - mine[b], axis, False)

    def arrived(hot, b, keep, other):
        return jnp.where(((me ^ hot) >> b) & 1 == 1, other, keep)

    inverse = 1.0 / (eigen_out[None, :, None] * eigen_in.reshape(TILES, GROUPED).T[:, None, :] + damping[0])
    other = across(send, 0)
    keep, other = (x.reshape((EXTRA,) + (2,) * (bits - 1) + (share, COLS)) for x in (keep, other))
    chains = []
    for rank in range(hot_total):
        rest = list(range(1, bits))
        turn = rank % 2
        steps = rest[turn : turn + 1] + rest[:turn] + rest[turn + 1 :]
        chains.append([arrived(hots[rank], 0, keep, other), steps, rest])

    for k in range(bits - 1):
        parts = [halves(x, steps[k], left) for x, steps, left in chains]
        sends = [part[1] for part in parts]
        if k == 0:
            *sends, inverse = lax.optimization_barrier((*sends, inverse))
            conditioned = precondition(train_features, basis_in, basis_out, inverse.reshape(WIDE, TILES), devices)
            conditioned, first_share = lax.optimization_barrier((conditioned, first_share))
            train_share = to_all(conditioned)
        if k == bits - 2:
            *sends, train_share = lax.optimization_barrier((*sends, train_share))
        others = [across(send, chain[1][k]) for send, chain in zip(sends, chains)]
        others = lax.optimization_barrier(others)
        for rank, chain in enumerate(chains):
            chain[0] = arrived(hots[rank], chain[1][k], parts[rank][0], others[rank])
    extra_share = jnp.concatenate([chain[0] for chain in chains], axis=0)

    rows = jnp.concatenate([rows, jnp.broadcast_to(mine[0], (1, rows.shape[1]))])
    keep, send = partial_scores(rows, per_device, train_share, first_share, extra_share)
    tiles = keep + across(send, 0)
    tiles = tiles.reshape((2,) * (bits - 1) + (per_device, COLS, COLS))
    sums, middle = [], list(range(1, bits - 1))
    for pair in range(per_device):
        x, left = tiles[..., pair, :, :], list(range(1, bits))
        turn = pair % 2
        for k, b in enumerate(middle[turn:] + middle[:turn]):
            axis = sorted(left, reverse=True).index(b)
            left.remove(b)
            keep = lax.dynamic_index_in_dim(x, mine[b], axis, False)
            send = lax.dynamic_index_in_dim(x, 1 - mine[b], axis, False)
            if k == 0:
                x = keep + across(send.astype(bf16), b).astype(f32)
            else:
                x = keep + across(send, b)
        sums.append(x)
    tiles = jnp.stack(sums, axis=1)
    keep = lax.dynamic_index_in_dim(tiles, mine[-1], 0, False)
    send = lax.dynamic_index_in_dim(tiles, 1 - mine[-1], 0, False)
    tiles = keep + across(send, bits - 1)
    return tiles


def solution(mesh):
    placed = (
        P(None, ("groups", "dp")),
        P(None, ("groups", "dp")),
        P(("groups", "dp"), None),
        P("groups", None),
        P("groups", None),
        P("groups"),
        P("groups"),
        P("groups"),
    )
    return jax.shard_map(
        functools.partial(body, mesh.shape["dp"]),
        mesh=mesh,
        in_specs=placed,
        out_specs=P(("groups", "dp"), None, None),
        check_vma=False,
    )
```

```python
import functools

import jax
import jax.numpy as jnp
from jax import lax
from jax.experimental import pallas as pl
from jax.experimental.pallas import tpu as pltpu
from jax.sharding import PartitionSpec as P

SIDE = 64
COLS = 128
NAMED_MOST = 4
EXTRA = NAMED_MOST - 1
GROUPED = 4
WIDE = GROUPED * SIDE
TILES = SIDE // GROUPED
VMEM_LIMIT = 40 * 1024 * 1024
FULL_VMEM = 60 * 1024 * 1024
f32, bf16 = jnp.float32, jnp.bfloat16


def split(x):
    high = x.astype(bf16)
    return high, (x - high.astype(f32)).astype(bf16)


def mm(a, b):
    return jnp.dot(a, b, preferred_element_type=f32)


def mm_nt(a, b):
    return lax.dot_general(a, b, (((1,), (1,)), ((), ())), preferred_element_type=f32)


def mm3(a, b):
    return mm(a[0], b[0]) + (mm(a[0], b[1]) + mm(a[1], b[0]))


def iota(shape, axis):
    return lax.broadcasted_iota(jnp.int32, shape, axis)


def chosen(cond):
    return jnp.where(cond, 1.0, 0.0).astype(bf16)


def precondition_kernel(train, basis_in, basis_out, inverse, out, y_high, y_low, z_high, z_low):
    tall, flat, square = (WIDE, SIDE), (SIDE, WIDE), (WIDE, WIDE)
    pick_i = chosen(iota(tall, 0) // GROUPED == iota(tall, 1))
    pick_i_t = chosen(iota(flat, 1) // GROUPED == iota(flat, 0))
    pick_low = chosen(iota(tall, 0) % SIDE == iota(tall, 1))
    pick_low_t = chosen(iota(flat, 1) % SIDE == iota(flat, 0))
    row_a = iota(tall, 0) // (GROUPED * GROUPED) * GROUPED + iota(tall, 0) % GROUPED
    pick_a = chosen(row_a == iota(tall, 1))
    col_a = iota(flat, 1) // (GROUPED * GROUPED) * GROUPED + iota(flat, 1) % GROUPED
    pick_a_t = chosen(col_a == iota(flat, 0))
    r, c = iota(square, 0), iota(square, 1)
    same_in = r % GROUPED == c // SIDE
    same_in_t = c % GROUPED == r // SIDE
    same_out = r // GROUPED % GROUPED == c // SIDE
    same_out_t = c // GROUPED % GROUPED == r // SIDE

    def masked(cond, x):
        return jnp.where(cond, x, 0.0).astype(bf16)

    in_parts, out_parts = split(basis_in[...]), split(basis_out[...])
    w_in = [masked(same_in, mm(mm_nt(pick_i, b).astype(bf16), pick_low_t)) for b in in_parts]
    w_in_t = [masked(same_in_t, mm(mm(pick_low, b).astype(bf16), pick_i_t)) for b in in_parts]
    w_out = [masked(same_out, mm(mm(pick_a, b).astype(bf16), pick_low_t)) for b in out_parts]
    w_out_t = [masked(same_out_t, mm(mm_nt(pick_low, b).astype(bf16), pick_a_t)) for b in out_parts]

    for A in range(0, TILES, 2):
        x = jnp.concatenate([train[pl.ds((A + k) * WIDE, WIDE), :] for k in range(2)], axis=1)
        high, low = split(mm(w_in[0], x) + mm(w_in[1], x))
        for k in range(2):
            y_high[A + k] = high[:, k * COLS : (k + 1) * COLS].reshape(TILES, -1, COLS)
            y_low[A + k] = low[:, k * COLS : (k + 1) * COLS].reshape(TILES, -1, COLS)
    for g in range(0, TILES, 2):
        y = [jnp.concatenate([ref[:, g + k].reshape(WIDE, COLS) for k in range(2)], axis=1) for ref in (y_high, y_low)]
        s = mm3(w_out_t, y)
        factor = [jnp.broadcast_to(inverse[:, g + k : g + k + 1], (WIDE, COLS)) for k in range(2)]
        high, low = split(mm3(w_out, split(s * jnp.concatenate(factor, axis=1))))
        for k in range(2):
            z_high[:, g + k] = high[:, k * COLS : (k + 1) * COLS].reshape(TILES, -1, COLS)
            z_low[:, g + k] = low[:, k * COLS : (k + 1) * COLS].reshape(TILES, -1, COLS)
    share = out.shape[2]
    for A in range(0, TILES, 2):
        z = [jnp.concatenate([ref[A + k].reshape(WIDE, COLS) for k in range(2)], axis=1) for ref in (z_high, z_low)]
        result = mm3(w_in_t, z)
        for k in range(2):
            turned = result[:, k * COLS : (k + 1) * COLS].T.astype(bf16)
            for part in range(WIDE // share):
                out[(A + k) * (WIDE // share) + part] = turned[:, part * share : (part + 1) * share]


def precondition(train, basis_in, basis_out, inverse, chunks):
    features = train.shape[0]
    tiled = pltpu.VMEM((TILES, TILES, WIDE // TILES, COLS), bf16)
    return pl.pallas_call(
        precondition_kernel,
        out_shape=jax.ShapeDtypeStruct((chunks, COLS, features // chunks), bf16),
        in_specs=[pl.BlockSpec(memory_space=pltpu.VMEM)] * 4,
        out_specs=pl.BlockSpec(memory_space=pltpu.VMEM),
        scratch_shapes=[tiled] * 4,
        compiler_params=pltpu.CompilerParams(vmem_limit_bytes=VMEM_LIMIT),
        cost_estimate=pl.CostEstimate(flops=3_000_000_000, bytes_accessed=4 * features * COLS, transcendentals=0),
        name="precondition",
    )(train, basis_in, basis_out, inverse)


def came_across(me, where, hot, bit):
    return lax.shift_right_logical(me[0] ^ where[hot], bit) & 1


def pick_kernel(plan_of, me, where, *refs):
    count = len(plan_of)
    sources, outs = refs[: 2 * count], refs[2 * count :]
    for hot, (bit, next_bit) in enumerate(plan_of):
        mine = lax.shift_right_logical(me[0], next_bit) & 1
        across = came_across(me, where, hot, bit)
        for way in range(2):
            source = sources[2 * hot + way]

            @pl.when(across == way)
            def _():
                for k in range(source.shape[0]):
                    outs[2 * hot][k] = source[k, mine]
                    outs[2 * hot + 1][k] = source[k, 1 - mine]


def pick(me, where, sources, plan_of):
    whole = pl.BlockSpec(memory_space=pltpu.VMEM)
    shapes = [jax.ShapeDtypeStruct(x.shape[:1] + x.shape[2:], x.dtype) for x in sources]
    return pl.pallas_call(
        functools.partial(pick_kernel, plan_of),
        out_shape=shapes,
        in_specs=[pl.BlockSpec(memory_space=pltpu.SMEM)] * 2 + [whole] * len(sources),
        out_specs=[whole] * len(shapes),
        compiler_params=pltpu.CompilerParams(vmem_limit_bytes=VMEM_LIMIT),
        name="pick",
    )(me.reshape(1), where, *sources)


def score_kernel(per_device, local_blocks, me_ref, pairs, masks, ranks, train, first, extra, keep, send):
    core = me_ref[0] & 1
    level = local_blocks.bit_length() - 1
    devices = first.shape[0]

    def tile(pair):
        block = pairs[pair, 1]
        d = lax.shift_right_logical(block, level)
        before = masks[d] & (lax.shift_left(1, block & (local_blocks - 1)) - 1)
        order = before & 1
        for k in range(1, local_blocks):
            order = order + (lax.shift_right_logical(before, k) & 1)
        slot = jnp.where(order == 0, d, devices + EXTRA * ranks[d] + order - 1)
        a = first[jnp.minimum(slot, devices - 1)]
        b = extra[jnp.maximum(slot - devices, 0)]
        q = jnp.where(slot < devices, a.astype(f32), b.astype(f32)).astype(bf16)
        return mm(train[pairs[pair, 0]], q)

    def step(h, carry):
        base = h // per_device * (2 * per_device) + h % per_device
        keep[h] = tile(base + core * per_device)
        send[h] = tile(base + (1 - core) * per_device)
        return carry

    lax.fori_loop(0, keep.shape[0], step, 0, unroll=4)


def partial_scores(per_device, local_blocks, me, pairs, masks, ranks, train, first, extra):
    half = pairs.shape[0] // 2
    tiles = jax.ShapeDtypeStruct((half, COLS, COLS), f32)
    whole = pl.BlockSpec(memory_space=pltpu.VMEM)
    return pl.pallas_call(
        functools.partial(score_kernel, per_device, local_blocks),
        out_shape=(tiles, tiles),
        in_specs=[pl.BlockSpec(memory_space=pltpu.SMEM)] * 4 + [whole] * 3,
        out_specs=(whole, whole),
        compiler_params=pltpu.CompilerParams(vmem_limit_bytes=VMEM_LIMIT),
        name="partial_scores",
    )(me.reshape(1), pairs, masks, ranks, train, first, extra)


def plan_kernel(
    me_ref, pairs, query, masks, ranks, hots, first, keep, send, own, first_sem, keep_sem, send_sem
):
    me = me_ref[0]
    devices, total = masks.shape[0], pairs.shape[0]
    local_blocks = query.shape[3] // COLS
    level = local_blocks.bit_length() - 1

    @pl.loop(0, devices, unroll=8)
    def _(d):
        masks[d] = 0

    @pl.loop(0, total, unroll=8)
    def _(p):
        block = pairs[p, 1]
        d = lax.shift_right_logical(block, level)
        masks[d] = masks[d] | lax.shift_left(1, block & (local_blocks - 1))

    count = jnp.int32(0)
    mask = masks[me]
    for k in range(local_blocks):
        bit = lax.shift_right_logical(mask, k) & 1

        @pl.when(bit == 1)
        def _():
            own[jnp.minimum(count, EXTRA)] = k

        count = count + bit
    is_hot = count > 1

    def cut(k, source, target, sem):
        start = pl.multiple_of(own[k] * COLS, COLS)
        return pltpu.make_async_copy(source.at[..., pl.ds(start, COLS)], target, sem)

    core = me & 1
    parts = first_sem.shape[0]
    length = query.shape[0] // parts

    def first_copies(part):
        at = pl.ds(part * length, length)
        return cut(0, query.at[at], first.at[at], first_sem.at[part])

    for part in range(parts):
        first_copies(part).start()

    def extra_copies(k):
        return (
            cut(k + 1, query.at[:, core], keep.at[k], keep_sem.at[k]),
            cut(k + 1, query.at[:, 1 - core], send.at[k], send_sem.at[k]),
        )

    @pl.when(is_hot)
    def _():
        for k in range(EXTRA):
            for copy in extra_copies(k):
                copy.start()

    def rank_step(d, rank):
        mask = masks[d]
        hot = (mask & (mask - 1)) != 0

        ranks[d] = rank

        @pl.when(hot)
        def _():
            hots[jnp.minimum(rank, hots.shape[0] - 1)] = d

        return rank + jnp.where(hot, 1, 0)

    lax.fori_loop(0, devices, rank_step, jnp.int32(0), unroll=4)

    for part in range(parts):
        first_copies(part).wait()

    @pl.when(is_hot)
    def _():
        for k in range(EXTRA):
            for copy in extra_copies(k):
                copy.wait()


def plan(me, pairs, query, devices, share, hot_total):
    smem, hbm = pl.BlockSpec(memory_space=pltpu.SMEM), pl.BlockSpec(memory_space=pl.ANY)
    vmem = pl.BlockSpec(memory_space=pltpu.VMEM)
    half = devices // 2
    extra = jax.ShapeDtypeStruct((EXTRA, half, share, COLS), bf16)
    return pl.pallas_call(
        plan_kernel,
        out_shape=(
            jax.ShapeDtypeStruct((devices,), jnp.int32),
            jax.ShapeDtypeStruct((devices,), jnp.int32),
            jax.ShapeDtypeStruct((hot_total,), jnp.int32),
            jax.ShapeDtypeStruct((half, 2, share, COLS), bf16),
            extra,
            extra,
        ),
        in_specs=[smem, smem, hbm],
        out_specs=(smem, smem, smem, vmem, vmem, vmem),
        scratch_shapes=[
            pltpu.SMEM((NAMED_MOST,), jnp.int32),
            pltpu.SemaphoreType.DMA((8,)),
            pltpu.SemaphoreType.DMA((EXTRA,)),
            pltpu.SemaphoreType.DMA((EXTRA,)),
        ],
        compiler_params=pltpu.CompilerParams(vmem_limit_bytes=FULL_VMEM),
        name="plan",
    )(me.reshape(1), pairs, query.reshape(half, 2, share, -1))


def body(devices, train_features, query_gradients, block_pairs, basis_out, basis_in, eigen_out, eigen_in, damping):
    bits = devices.bit_length() - 1
    me = lax.axis_index("dp").astype(jnp.int32)
    mine = [(me >> b) & 1 for b in range(bits)]
    per_device = block_pairs.shape[0]
    share = query_gradients.shape[0] // devices
    hot_total = devices // 8

    def across(x, b):
        return lax.ppermute(x, "dp", [(d, d ^ (1 << b)) for d in range(devices)])

    def to_all(x):
        return lax.all_to_all(x, "dp", split_axis=0, concat_axis=0, tiled=True)

    pairs = block_pairs
    for b in range(bits):
        other = across(pairs, b)
        pairs = jnp.where(mine[b] == 0, jnp.concatenate([pairs, other]), jnp.concatenate([other, pairs]))

    masks, ranks, hots, first, keep, send = plan(me, pairs, query_gradients, devices, share, hot_total)
    first_share = to_all(first.reshape(devices, share, COLS))
    def halves(x, b, left):
        axis = 1 + sorted(left, reverse=True).index(b)
        left.remove(b)
        keep = lax.dynamic_index_in_dim(x, mine[b], axis, False)
        return keep, lax.dynamic_index_in_dim(x, 1 - mine[b], axis, False)

    def arrived(hot, b, keep, other):
        return jnp.where(((me ^ hot) >> b) & 1 == 1, other, keep)

    inverse = 1.0 / (eigen_out[None, :, None] * eigen_in.reshape(TILES, GROUPED).T[:, None, :] + damping[0])
    other = across(send, 0)
    keep, other = (x.reshape((EXTRA,) + (2,) * (bits - 1) + (share, COLS)) for x in (keep, other))
    chains = []
    for rank in range(hot_total):
        rest = list(range(1, bits))
        turn = rank % 2
        steps = rest[turn : turn + 1] + rest[:turn] + rest[turn + 1 :]
        chains.append([keep, other, 0, steps, rest])

    for k in range(bits - 1):
        if k in (0,):
            sources, plan_of = [], []
            for keep, other, bit, steps, left in chains:
                before = EXTRA * 2 ** sorted(left, reverse=True).index(steps[k])
                sources += [x.reshape(before, 2, -1, COLS) for x in (keep, other)]
                plan_of.append((bit, steps[k]))
                left.remove(steps[k])
            halved = pick(me, hots, sources, tuple(plan_of))
            parts = [
                [x.reshape((EXTRA,) + (2,) * len(chain[4]) + (share, COLS)) for x in halved[2 * r : 2 * r + 2]]
                for r, chain in enumerate(chains)
            ]
        else:
            parts = []
            for rank, (keep, other, bit, steps, left) in enumerate(chains):
                parts.append(halves(arrived(hots[rank], bit, keep, other), steps[k], left))
        sends = [part[1] for part in parts]
        if k == 0:
            *sends, inverse = lax.optimization_barrier((*sends, inverse))
            conditioned = precondition(train_features, basis_in, basis_out, inverse.reshape(WIDE, TILES), devices)
            conditioned, first_share = lax.optimization_barrier((conditioned, first_share))
            train_share = to_all(conditioned)
        if k == bits - 2:
            *sends, train_share = lax.optimization_barrier((*sends, train_share))
        others = [across(send, chain[3][k]) for send, chain in zip(sends, chains)]
        others = lax.optimization_barrier(others)
        for rank, chain in enumerate(chains):
            chain[:3] = parts[rank][0], others[rank], chain[3][k]
    extra_share = jnp.concatenate([arrived(hots[r], chain[2], chain[0], chain[1]) for r, chain in enumerate(chains)])

    local_blocks = query_gradients.shape[1] // COLS
    keep, send = partial_scores(
        per_device, local_blocks, me, pairs, masks, ranks, train_share, first_share, extra_share
    )
    tiles = keep + across(send, 0)
    tiles = tiles.reshape((2,) * (bits - 1) + (per_device, COLS, COLS))
    sums, middle = [], list(range(1, bits - 1))
    for pair in range(per_device):
        x, left = tiles[..., pair, :, :], list(range(1, bits))
        turn = pair % 2
        for k, b in enumerate(middle[turn:] + middle[:turn]):
            axis = sorted(left, reverse=True).index(b)
            left.remove(b)
            keep = lax.dynamic_index_in_dim(x, mine[b], axis, False)
            send = lax.dynamic_index_in_dim(x, 1 - mine[b], axis, False)
            if k == 0:
                x = keep + across(send.astype(bf16), b).astype(f32)
            else:
                x = keep + across(send, b)
        sums.append(x)
    tiles = jnp.stack(sums, axis=1)
    keep = lax.dynamic_index_in_dim(tiles, mine[-1], 0, False)
    send = lax.dynamic_index_in_dim(tiles, 1 - mine[-1], 0, False)
    tiles = keep + across(send, bits - 1)
    return tiles


def solution(mesh):
    placed = (
        P(None, ("groups", "dp")),
        P(None, ("groups", "dp")),
        P(("groups", "dp"), None),
        P("groups", None),
        P("groups", None),
        P("groups"),
        P("groups"),
        P("groups"),
    )
    return jax.shard_map(
        functools.partial(body, mesh.shape["dp"]),
        mesh=mesh,
        in_specs=placed,
        out_specs=P(("groups", "dp"), None, None),
        check_vma=False,
    )
```

```python
import functools

import jax
import jax.numpy as jnp
from jax import lax
from jax.experimental import pallas as pl
from jax.experimental.pallas import tpu as pltpu
from jax.sharding import PartitionSpec as P

SIDE = 64
COLS = 128
NAMED_MOST = 4
EXTRA = NAMED_MOST - 1
GROUPED = 4
WIDE = GROUPED * SIDE
TILES = SIDE // GROUPED
VMEM_LIMIT = 40 * 1024 * 1024
FULL_VMEM = 60 * 1024 * 1024
f32, bf16 = jnp.float32, jnp.bfloat16


def split(x):
    high = x.astype(bf16)
    return high, (x - high.astype(f32)).astype(bf16)


def mm(a, b):
    return jnp.dot(a, b, preferred_element_type=f32)


def mm_nt(a, b):
    return lax.dot_general(a, b, (((1,), (1,)), ((), ())), preferred_element_type=f32)


def mm3(a, b):
    return mm(a[0], b[0]) + (mm(a[0], b[1]) + mm(a[1], b[0]))


def iota(shape, axis):
    return lax.broadcasted_iota(jnp.int32, shape, axis)


def chosen(cond):
    return jnp.where(cond, 1.0, 0.0).astype(bf16)


def precondition_kernel(train, basis_in, basis_out, inverse, out, y_high, y_low, z_high, z_low):
    tall, flat, square = (WIDE, SIDE), (SIDE, WIDE), (WIDE, WIDE)
    pick_i = chosen(iota(tall, 0) // GROUPED == iota(tall, 1))
    pick_i_t = chosen(iota(flat, 1) // GROUPED == iota(flat, 0))
    pick_low = chosen(iota(tall, 0) % SIDE == iota(tall, 1))
    pick_low_t = chosen(iota(flat, 1) % SIDE == iota(flat, 0))
    row_a = iota(tall, 0) // (GROUPED * GROUPED) * GROUPED + iota(tall, 0) % GROUPED
    pick_a = chosen(row_a == iota(tall, 1))
    col_a = iota(flat, 1) // (GROUPED * GROUPED) * GROUPED + iota(flat, 1) % GROUPED
    pick_a_t = chosen(col_a == iota(flat, 0))
    r, c = iota(square, 0), iota(square, 1)
    same_in = r % GROUPED == c // SIDE
    same_in_t = c % GROUPED == r // SIDE
    same_out = r // GROUPED % GROUPED == c // SIDE
    same_out_t = c // GROUPED % GROUPED == r // SIDE

    def masked(cond, x):
        return jnp.where(cond, x, 0.0).astype(bf16)

    in_parts, out_parts = split(basis_in[...]), split(basis_out[...])
    w_in = [masked(same_in, mm(mm_nt(pick_i, b).astype(bf16), pick_low_t)) for b in in_parts]
    w_in_t = [masked(same_in_t, mm(mm(pick_low, b).astype(bf16), pick_i_t)) for b in in_parts]
    w_out = [masked(same_out, mm(mm(pick_a, b).astype(bf16), pick_low_t)) for b in out_parts]
    w_out_t = [masked(same_out_t, mm(mm_nt(pick_low, b).astype(bf16), pick_a_t)) for b in out_parts]

    for A in range(0, TILES, 2):
        x = jnp.concatenate([train[pl.ds((A + k) * WIDE, WIDE), :] for k in range(2)], axis=1)
        high, low = split(mm(w_in[0], x) + mm(w_in[1], x))
        for k in range(2):
            y_high[A + k] = high[:, k * COLS : (k + 1) * COLS].reshape(TILES, -1, COLS)
            y_low[A + k] = low[:, k * COLS : (k + 1) * COLS].reshape(TILES, -1, COLS)
    for g in range(0, TILES, 2):
        y = [jnp.concatenate([ref[:, g + k].reshape(WIDE, COLS) for k in range(2)], axis=1) for ref in (y_high, y_low)]
        s = mm3(w_out_t, y)
        factor = [jnp.broadcast_to(inverse[:, g + k : g + k + 1], (WIDE, COLS)) for k in range(2)]
        high, low = split(mm3(w_out, split(s * jnp.concatenate(factor, axis=1))))
        for k in range(2):
            z_high[:, g + k] = high[:, k * COLS : (k + 1) * COLS].reshape(TILES, -1, COLS)
            z_low[:, g + k] = low[:, k * COLS : (k + 1) * COLS].reshape(TILES, -1, COLS)
    share = out.shape[2]
    for A in range(0, TILES, 2):
        z = [jnp.concatenate([ref[A + k].reshape(WIDE, COLS) for k in range(2)], axis=1) for ref in (z_high, z_low)]
        result = mm3(w_in_t, z)
        for k in range(2):
            turned = result[:, k * COLS : (k + 1) * COLS].T.astype(bf16)
            for part in range(WIDE // share):
                out[(A + k) * (WIDE // share) + part] = turned[:, part * share : (part + 1) * share]


def precondition(train, basis_in, basis_out, inverse, chunks):
    features = train.shape[0]
    tiled = pltpu.VMEM((TILES, TILES, WIDE // TILES, COLS), bf16)
    return pl.pallas_call(
        precondition_kernel,
        out_shape=jax.ShapeDtypeStruct((chunks, COLS, features // chunks), bf16),
        in_specs=[pl.BlockSpec(memory_space=pltpu.VMEM)] * 4,
        out_specs=pl.BlockSpec(memory_space=pltpu.VMEM),
        scratch_shapes=[tiled] * 4,
        compiler_params=pltpu.CompilerParams(vmem_limit_bytes=VMEM_LIMIT),
        cost_estimate=pl.CostEstimate(flops=3_000_000_000, bytes_accessed=4 * features * COLS, transcendentals=0),
        name="precondition",
    )(train, basis_in, basis_out, inverse)


def came_across(me, where, hot, bit):
    return lax.shift_right_logical(me[0] ^ where[hot], bit) & 1


def pick_kernel(plan_of, me, where, *refs):
    count = len(plan_of)
    sources, outs = refs[: 2 * count], refs[2 * count :]
    for hot, (bit, next_bit) in enumerate(plan_of):
        mine = lax.shift_right_logical(me[0], next_bit) & 1
        across = came_across(me, where, hot, bit)
        for way in range(2):
            source = sources[2 * hot + way]

            @pl.when(across == way)
            def _():
                for k in range(source.shape[0]):
                    outs[2 * hot][k] = source[k, mine]
                    outs[2 * hot + 1][k] = source[k, 1 - mine]


def pick(me, where, sources, plan_of):
    whole = pl.BlockSpec(memory_space=pltpu.VMEM)
    shapes = [jax.ShapeDtypeStruct(x.shape[:1] + x.shape[2:], x.dtype) for x in sources]
    return pl.pallas_call(
        functools.partial(pick_kernel, plan_of),
        out_shape=shapes,
        in_specs=[pl.BlockSpec(memory_space=pltpu.SMEM)] * 2 + [whole] * len(sources),
        out_specs=[whole] * len(shapes),
        compiler_params=pltpu.CompilerParams(vmem_limit_bytes=VMEM_LIMIT),
        name="pick",
    )(me.reshape(1), where, *sources)


def score_kernel(which, per_device, me_ref, rows, train, first, extra, keep, send):
    core = me_ref[0] & 1
    devices = first.shape[0]

    def tile(device):
        pair = device * per_device + which
        slot = rows[1, pair]
        a = first[jnp.minimum(slot, devices - 1)]
        b = extra[jnp.maximum(slot - devices, 0)]
        q = jnp.where(slot < devices, a.astype(f32), b.astype(f32)).astype(bf16)
        return mm(train[rows[0, pair]], q)

    def step(h, carry):
        keep[h] = tile(2 * h + core)
        send[h] = tile(2 * h + 1 - core)
        return carry

    lax.fori_loop(0, keep.shape[0], step, 0, unroll=4)


def partial_scores(which, per_device, me, rows, train, first, extra):
    half = rows.shape[1] // (2 * per_device)
    tiles = jax.ShapeDtypeStruct((half, COLS, COLS), f32)
    whole = pl.BlockSpec(memory_space=pltpu.VMEM)
    return pl.pallas_call(
        functools.partial(score_kernel, which, per_device),
        out_shape=(tiles, tiles),
        in_specs=[pl.BlockSpec(memory_space=pltpu.SMEM)] * 2 + [whole] * 3,
        out_specs=(whole, whole),
        compiler_params=pltpu.CompilerParams(vmem_limit_bytes=VMEM_LIMIT),
        name="partial_scores",
    )(me.reshape(1), rows, train, first, extra)


def plan_kernel(
    me_ref, pairs, query, rows, hots, first, keep, send, masks, ranks, own, first_sem, keep_sem, send_sem
):
    me = me_ref[0]
    devices, total = masks.shape[0], pairs.shape[0]
    local_blocks = query.shape[3] // COLS
    level = local_blocks.bit_length() - 1

    @pl.loop(0, devices, unroll=8)
    def _(d):
        masks[d] = 0

    @pl.loop(0, total, unroll=8)
    def _(p):
        block = pairs[p, 1]
        d = lax.shift_right_logical(block, level)
        masks[d] = masks[d] | lax.shift_left(1, block & (local_blocks - 1))

    count = jnp.int32(0)
    mask = masks[me]
    for k in range(local_blocks):
        bit = lax.shift_right_logical(mask, k) & 1

        @pl.when(bit == 1)
        def _():
            own[jnp.minimum(count, EXTRA)] = k

        count = count + bit
    is_hot = count > 1

    def cut(k, source, target, sem):
        start = pl.multiple_of(own[k] * COLS, COLS)
        return pltpu.make_async_copy(source.at[..., pl.ds(start, COLS)], target, sem)

    core = me & 1
    parts = first_sem.shape[0]
    length = query.shape[0] // parts

    def first_copies(part):
        at = pl.ds(part * length, length)
        return cut(0, query.at[at], first.at[at], first_sem.at[part])

    for part in range(parts):
        first_copies(part).start()

    def extra_copies(k):
        return (
            cut(k + 1, query.at[:, core], keep.at[k], keep_sem.at[k]),
            cut(k + 1, query.at[:, 1 - core], send.at[k], send_sem.at[k]),
        )

    @pl.when(is_hot)
    def _():
        for k in range(EXTRA):
            for copy in extra_copies(k):
                copy.start()

    def rank_step(d, rank):
        mask = masks[d]
        hot = (mask & (mask - 1)) != 0

        ranks[d] = rank

        @pl.when(hot)
        def _():
            hots[jnp.minimum(rank, hots.shape[0] - 1)] = d

        return rank + jnp.where(hot, 1, 0)

    lax.fori_loop(0, devices, rank_step, jnp.int32(0), unroll=4)

    @pl.loop(0, total, unroll=4)
    def _(p):
        block = pairs[p, 1]
        d = lax.shift_right_logical(block, level)
        before = masks[d] & (lax.shift_left(1, block & (local_blocks - 1)) - 1)
        order = before & 1
        for k in range(1, local_blocks):
            order = order + (lax.shift_right_logical(before, k) & 1)
        rows[0, p] = pairs[p, 0]
        rows[1, p] = jnp.where(order == 0, d, devices + EXTRA * ranks[d] + order - 1)

    for part in range(parts):
        first_copies(part).wait()

    @pl.when(is_hot)
    def _():
        for k in range(EXTRA):
            for copy in extra_copies(k):
                copy.wait()


def plan(me, pairs, query, devices, share, hot_total):
    smem, hbm = pl.BlockSpec(memory_space=pltpu.SMEM), pl.BlockSpec(memory_space=pl.ANY)
    vmem = pl.BlockSpec(memory_space=pltpu.VMEM)
    half = devices // 2
    extra = jax.ShapeDtypeStruct((EXTRA, half, share, COLS), bf16)
    return pl.pallas_call(
        plan_kernel,
        out_shape=(
            jax.ShapeDtypeStruct((2, pairs.shape[0]), jnp.int32),
            jax.ShapeDtypeStruct((hot_total,), jnp.int32),
            jax.ShapeDtypeStruct((half, 2, share, COLS), bf16),
            extra,
            extra,
        ),
        in_specs=[smem, smem, hbm],
        out_specs=(smem, smem, vmem, vmem, vmem),
        scratch_shapes=[
            pltpu.SMEM((devices,), jnp.int32),
            pltpu.SMEM((devices,), jnp.int32),
            pltpu.SMEM((NAMED_MOST,), jnp.int32),
            pltpu.SemaphoreType.DMA((8,)),
            pltpu.SemaphoreType.DMA((EXTRA,)),
            pltpu.SemaphoreType.DMA((EXTRA,)),
        ],
        compiler_params=pltpu.CompilerParams(vmem_limit_bytes=FULL_VMEM),
        name="plan",
    )(me.reshape(1), pairs, query.reshape(half, 2, share, -1))


def body(devices, train_features, query_gradients, block_pairs, basis_out, basis_in, eigen_out, eigen_in, damping):
    bits = devices.bit_length() - 1
    me = lax.axis_index("dp").astype(jnp.int32)
    mine = [(me >> b) & 1 for b in range(bits)]
    per_device = block_pairs.shape[0]
    share = query_gradients.shape[0] // devices
    hot_total = devices // 8

    def across(x, b):
        return lax.ppermute(x, "dp", [(d, d ^ (1 << b)) for d in range(devices)])

    def to_all(x):
        return lax.all_to_all(x, "dp", split_axis=0, concat_axis=0, tiled=True)

    pairs = block_pairs
    for b in range(bits):
        other = across(pairs, b)
        pairs = jnp.where(mine[b] == 0, jnp.concatenate([pairs, other]), jnp.concatenate([other, pairs]))

    rows, hots, first, keep, send = plan(me, pairs, query_gradients, devices, share, hot_total)
    first_share = to_all(first.reshape(devices, share, COLS))
    def halves(x, b, left):
        axis = 1 + sorted(left, reverse=True).index(b)
        left.remove(b)
        keep = lax.dynamic_index_in_dim(x, mine[b], axis, False)
        return keep, lax.dynamic_index_in_dim(x, 1 - mine[b], axis, False)

    def arrived(hot, b, keep, other):
        return jnp.where(((me ^ hot) >> b) & 1 == 1, other, keep)

    inverse = 1.0 / (eigen_out[None, :, None] * eigen_in.reshape(TILES, GROUPED).T[:, None, :] + damping[0])
    other = across(send, 0)
    keep, other = (x.reshape((EXTRA,) + (2,) * (bits - 1) + (share, COLS)) for x in (keep, other))
    chains = []
    for rank in range(hot_total):
        rest = list(range(1, bits))
        turn = rank % 2
        steps = rest[turn : turn + 1] + rest[:turn] + rest[turn + 1 :]
        chains.append([keep, other, 0, steps, rest])

    for k in range(bits - 1):
        if k in (0,):
            sources, plan_of = [], []
            for keep, other, bit, steps, left in chains:
                before = EXTRA * 2 ** sorted(left, reverse=True).index(steps[k])
                sources += [x.reshape(before, 2, -1, COLS) for x in (keep, other)]
                plan_of.append((bit, steps[k]))
                left.remove(steps[k])
            halved = pick(me, hots, sources, tuple(plan_of))
            parts = [
                [x.reshape((EXTRA,) + (2,) * len(chain[4]) + (share, COLS)) for x in halved[2 * r : 2 * r + 2]]
                for r, chain in enumerate(chains)
            ]
        else:
            parts = []
            for rank, (keep, other, bit, steps, left) in enumerate(chains):
                parts.append(halves(arrived(hots[rank], bit, keep, other), steps[k], left))
        sends = [part[1] for part in parts]
        if k == 0:
            *sends, inverse = lax.optimization_barrier((*sends, inverse))
            conditioned = precondition(train_features, basis_in, basis_out, inverse.reshape(WIDE, TILES), devices)
            conditioned, first_share = lax.optimization_barrier((conditioned, first_share))
            train_share = to_all(conditioned)
        if k == bits - 2:
            *sends, train_share = lax.optimization_barrier((*sends, train_share))
        others = [across(send, chain[3][k]) for send, chain in zip(sends, chains)]
        others = lax.optimization_barrier(others)
        for rank, chain in enumerate(chains):
            chain[:3] = parts[rank][0], others[rank], chain[3][k]
    extra_share = jnp.concatenate([arrived(hots[r], chain[2], chain[0], chain[1]) for r, chain in enumerate(chains)])

    sums, middle = [], list(range(1, bits - 1))
    for pair in range(per_device):
        keep, send = partial_scores(pair, per_device, me, rows, train_share, first_share, extra_share)
        x, left = (keep + across(send, 0)).reshape((2,) * (bits - 1) + (COLS, COLS)), list(range(1, bits))
        turn = pair % 2
        for k, b in enumerate(middle[turn:] + middle[:turn]):
            axis = sorted(left, reverse=True).index(b)
            left.remove(b)
            keep = lax.dynamic_index_in_dim(x, mine[b], axis, False)
            send = lax.dynamic_index_in_dim(x, 1 - mine[b], axis, False)
            if k == 0:
                x = keep + across(send.astype(bf16), b).astype(f32)
            else:
                x = keep + across(send, b)
        sums.append(x)
    tiles = jnp.stack(sums, axis=1)
    keep = lax.dynamic_index_in_dim(tiles, mine[-1], 0, False)
    send = lax.dynamic_index_in_dim(tiles, 1 - mine[-1], 0, False)
    tiles = keep + across(send, bits - 1)
    return tiles


def solution(mesh):
    placed = (
        P(None, ("groups", "dp")),
        P(None, ("groups", "dp")),
        P(("groups", "dp"), None),
        P("groups", None),
        P("groups", None),
        P("groups"),
        P("groups"),
        P("groups"),
    )
    return jax.shard_map(
        functools.partial(body, mesh.shape["dp"]),
        mesh=mesh,
        in_specs=placed,
        out_specs=P(("groups", "dp"), None, None),
        check_vma=False,
    )
```

```python
import functools

import jax
import jax.numpy as jnp
from jax import lax
from jax.experimental import pallas as pl
from jax.experimental.pallas import tpu as pltpu
from jax.sharding import PartitionSpec as P

SIDE = 64
COLS = 128
NAMED_MOST = 4
EXTRA = NAMED_MOST - 1
GROUPED = 4
WIDE = GROUPED * SIDE
TILES = SIDE // GROUPED
VMEM_LIMIT = 40 * 1024 * 1024
FULL_VMEM = 60 * 1024 * 1024
f32, bf16 = jnp.float32, jnp.bfloat16


def split(x):
    high = x.astype(bf16)
    return high, (x - high.astype(f32)).astype(bf16)


def mm(a, b):
    return jnp.dot(a, b, preferred_element_type=f32)


def mm_nt(a, b):
    return lax.dot_general(a, b, (((1,), (1,)), ((), ())), preferred_element_type=f32)


def mm3(a, b):
    return mm(a[0], b[0]) + (mm(a[0], b[1]) + mm(a[1], b[0]))


def iota(shape, axis):
    return lax.broadcasted_iota(jnp.int32, shape, axis)


def chosen(cond):
    return jnp.where(cond, 1.0, 0.0).astype(bf16)


def precondition_kernel(train, basis_in, basis_out, inverse, out, y_high, y_low, z_high, z_low):
    tall, flat, square = (WIDE, SIDE), (SIDE, WIDE), (WIDE, WIDE)
    pick_i = chosen(iota(tall, 0) // GROUPED == iota(tall, 1))
    pick_i_t = chosen(iota(flat, 1) // GROUPED == iota(flat, 0))
    pick_low = chosen(iota(tall, 0) % SIDE == iota(tall, 1))
    pick_low_t = chosen(iota(flat, 1) % SIDE == iota(flat, 0))
    row_a = iota(tall, 0) // (GROUPED * GROUPED) * GROUPED + iota(tall, 0) % GROUPED
    pick_a = chosen(row_a == iota(tall, 1))
    col_a = iota(flat, 1) // (GROUPED * GROUPED) * GROUPED + iota(flat, 1) % GROUPED
    pick_a_t = chosen(col_a == iota(flat, 0))
    r, c = iota(square, 0), iota(square, 1)
    same_in = r % GROUPED == c // SIDE
    same_in_t = c % GROUPED == r // SIDE
    same_out = r // GROUPED % GROUPED == c // SIDE
    same_out_t = c // GROUPED % GROUPED == r // SIDE

    def masked(cond, x):
        return jnp.where(cond, x, 0.0).astype(bf16)

    in_parts, out_parts = split(basis_in[...]), split(basis_out[...])
    w_in = [masked(same_in, mm(mm_nt(pick_i, b).astype(bf16), pick_low_t)) for b in in_parts]
    w_in_t = [masked(same_in_t, mm(mm(pick_low, b).astype(bf16), pick_i_t)) for b in in_parts]
    w_out = [masked(same_out, mm(mm(pick_a, b).astype(bf16), pick_low_t)) for b in out_parts]
    w_out_t = [masked(same_out_t, mm(mm_nt(pick_low, b).astype(bf16), pick_a_t)) for b in out_parts]

    for A in range(0, TILES, 2):
        x = jnp.concatenate([train[pl.ds((A + k) * WIDE, WIDE), :] for k in range(2)], axis=1)
        high, low = split(mm(w_in[0], x) + mm(w_in[1], x))
        for k in range(2):
            y_high[A + k] = high[:, k * COLS : (k + 1) * COLS].reshape(TILES, -1, COLS)
            y_low[A + k] = low[:, k * COLS : (k + 1) * COLS].reshape(TILES, -1, COLS)
    for g in range(0, TILES, 2):
        y = [jnp.concatenate([ref[:, g + k].reshape(WIDE, COLS) for k in range(2)], axis=1) for ref in (y_high, y_low)]
        s = mm3(w_out_t, y)
        factor = [jnp.broadcast_to(inverse[:, g + k : g + k + 1], (WIDE, COLS)) for k in range(2)]
        high, low = split(mm3(w_out, split(s * jnp.concatenate(factor, axis=1))))
        for k in range(2):
            z_high[:, g + k] = high[:, k * COLS : (k + 1) * COLS].reshape(TILES, -1, COLS)
            z_low[:, g + k] = low[:, k * COLS : (k + 1) * COLS].reshape(TILES, -1, COLS)
    share = out.shape[2]
    for A in range(0, TILES, 2):
        z = [jnp.concatenate([ref[A + k].reshape(WIDE, COLS) for k in range(2)], axis=1) for ref in (z_high, z_low)]
        result = mm3(w_in_t, z)
        for k in range(2):
            turned = result[:, k * COLS : (k + 1) * COLS].T.astype(bf16)
            for part in range(WIDE // share):
                out[(A + k) * (WIDE // share) + part] = turned[:, part * share : (part + 1) * share]


def precondition(train, basis_in, basis_out, inverse, chunks):
    features = train.shape[0]
    tiled = pltpu.VMEM((TILES, TILES, WIDE // TILES, COLS), bf16)
    return pl.pallas_call(
        precondition_kernel,
        out_shape=jax.ShapeDtypeStruct((chunks, COLS, features // chunks), bf16),
        in_specs=[pl.BlockSpec(memory_space=pltpu.VMEM)] * 4,
        out_specs=pl.BlockSpec(memory_space=pltpu.VMEM),
        scratch_shapes=[tiled] * 4,
        compiler_params=pltpu.CompilerParams(vmem_limit_bytes=VMEM_LIMIT),
        cost_estimate=pl.CostEstimate(flops=3_000_000_000, bytes_accessed=4 * features * COLS, transcendentals=0),
        name="precondition",
    )(train, basis_in, basis_out, inverse)


def came_across(me, where, hot, bit):
    return lax.shift_right_logical(me[0] ^ where[hot], bit) & 1


def pick_kernel(plan_of, me, where, *refs):
    count = len(plan_of)
    sources, outs = refs[: 2 * count], refs[2 * count :]
    for hot, (bit, next_bit) in enumerate(plan_of):
        mine = lax.shift_right_logical(me[0], next_bit) & 1
        across = came_across(me, where, hot, bit)
        for way in range(2):
            source = sources[2 * hot + way]

            @pl.when(across == way)
            def _():
                for k in range(source.shape[0]):
                    outs[2 * hot][k] = source[k, mine]
                    outs[2 * hot + 1][k] = source[k, 1 - mine]


def pick(me, where, sources, plan_of):
    whole = pl.BlockSpec(memory_space=pltpu.VMEM)
    shapes = [jax.ShapeDtypeStruct(x.shape[:1] + x.shape[2:], x.dtype) for x in sources]
    return pl.pallas_call(
        functools.partial(pick_kernel, plan_of),
        out_shape=shapes,
        in_specs=[pl.BlockSpec(memory_space=pltpu.SMEM)] * 2 + [whole] * len(sources),
        out_specs=[whole] * len(shapes),
        compiler_params=pltpu.CompilerParams(vmem_limit_bytes=VMEM_LIMIT),
        name="pick",
    )(me.reshape(1), where, *sources)


def score_kernel(per_device, me_ref, rows, train, first, extra, keep, send):
    core = me_ref[0] & 1
    devices = first.shape[0]

    def tile(pair):
        slot = rows[1, pair]
        a = first[jnp.minimum(slot, devices - 1)]
        b = extra[jnp.maximum(slot - devices, 0)]
        q = jnp.where(slot < devices, a.astype(f32), b.astype(f32)).astype(bf16)
        return mm(train[rows[0, pair]], q)

    def step(h, carry):
        base = h // per_device * (2 * per_device) + h % per_device
        keep[h] = tile(base + core * per_device)
        send[h] = tile(base + (1 - core) * per_device)
        return carry

    lax.fori_loop(0, keep.shape[0], step, 0, unroll=4)


def partial_scores(per_device, me, rows, train, first, extra):
    half = rows.shape[1] // 2
    tiles = jax.ShapeDtypeStruct((half, COLS, COLS), f32)
    whole = pl.BlockSpec(memory_space=pltpu.VMEM)
    return pl.pallas_call(
        functools.partial(score_kernel, per_device),
        out_shape=(tiles, tiles),
        in_specs=[pl.BlockSpec(memory_space=pltpu.SMEM)] * 2 + [whole] * 3,
        out_specs=(whole, whole),
        compiler_params=pltpu.CompilerParams(vmem_limit_bytes=VMEM_LIMIT),
        name="partial_scores",
    )(me.reshape(1), rows, train, first, extra)


def plan_kernel(
    me_ref, pairs, query, rows, hots, first, keep, send, masks, ranks, own, first_sem, keep_sem, send_sem
):
    me = me_ref[0]
    devices, total = masks.shape[0], pairs.shape[0]
    local_blocks = query.shape[3] // COLS
    level = local_blocks.bit_length() - 1

    @pl.loop(0, devices, unroll=8)
    def _(d):
        masks[d] = 0

    @pl.loop(0, total, unroll=8)
    def _(p):
        block = pairs[p, 1]
        d = lax.shift_right_logical(block, level)
        masks[d] = masks[d] | lax.shift_left(1, block & (local_blocks - 1))

    count = jnp.int32(0)
    mask = masks[me]
    for k in range(local_blocks):
        bit = lax.shift_right_logical(mask, k) & 1

        @pl.when(bit == 1)
        def _():
            own[jnp.minimum(count, EXTRA)] = k

        count = count + bit
    is_hot = count > 1

    def cut(k, source, target, sem):
        start = pl.multiple_of(own[k] * COLS, COLS)
        return pltpu.make_async_copy(source.at[..., pl.ds(start, COLS)], target, sem)

    core = me & 1
    parts = first_sem.shape[0]
    length = query.shape[0] // parts

    def first_copies(part):
        at = pl.ds(part * length, length)
        return cut(0, query.at[at], first.at[at], first_sem.at[part])

    for part in range(parts):
        first_copies(part).start()

    def extra_copies(k):
        return (
            cut(k + 1, query.at[:, core], keep.at[k], keep_sem.at[k]),
            cut(k + 1, query.at[:, 1 - core], send.at[k], send_sem.at[k]),
        )

    @pl.when(is_hot)
    def _():
        for k in range(EXTRA):
            for copy in extra_copies(k):
                copy.start()

    def rank_step(d, rank):
        mask = masks[d]
        hot = (mask & (mask - 1)) != 0

        ranks[d] = rank

        @pl.when(hot)
        def _():
            hots[jnp.minimum(rank, hots.shape[0] - 1)] = d

        return rank + jnp.where(hot, 1, 0)

    lax.fori_loop(0, devices, rank_step, jnp.int32(0), unroll=4)

    @pl.loop(0, total, unroll=4)
    def _(p):
        block = pairs[p, 1]
        d = lax.shift_right_logical(block, level)
        before = masks[d] & (lax.shift_left(1, block & (local_blocks - 1)) - 1)
        order = before & 1
        for k in range(1, local_blocks):
            order = order + (lax.shift_right_logical(before, k) & 1)
        rows[0, p] = pairs[p, 0]
        rows[1, p] = jnp.where(order == 0, d, devices + EXTRA * ranks[d] + order - 1)

    for part in range(parts):
        first_copies(part).wait()

    @pl.when(is_hot)
    def _():
        for k in range(EXTRA):
            for copy in extra_copies(k):
                copy.wait()


def plan(me, pairs, query, devices, share, hot_total):
    smem, hbm = pl.BlockSpec(memory_space=pltpu.SMEM), pl.BlockSpec(memory_space=pl.ANY)
    vmem = pl.BlockSpec(memory_space=pltpu.VMEM)
    half = devices // 2
    extra = jax.ShapeDtypeStruct((EXTRA, half, share, COLS), bf16)
    return pl.pallas_call(
        plan_kernel,
        out_shape=(
            jax.ShapeDtypeStruct((2, pairs.shape[0]), jnp.int32),
            jax.ShapeDtypeStruct((hot_total,), jnp.int32),
            jax.ShapeDtypeStruct((half, 2, share, COLS), bf16),
            extra,
            extra,
        ),
        in_specs=[smem, smem, hbm],
        out_specs=(smem, smem, vmem, vmem, vmem),
        scratch_shapes=[
            pltpu.SMEM((devices,), jnp.int32),
            pltpu.SMEM((devices,), jnp.int32),
            pltpu.SMEM((NAMED_MOST,), jnp.int32),
            pltpu.SemaphoreType.DMA((8,)),
            pltpu.SemaphoreType.DMA((EXTRA,)),
            pltpu.SemaphoreType.DMA((EXTRA,)),
        ],
        compiler_params=pltpu.CompilerParams(vmem_limit_bytes=FULL_VMEM),
        name="plan",
    )(me.reshape(1), pairs, query.reshape(half, 2, share, -1))


def body(devices, train_features, query_gradients, block_pairs, basis_out, basis_in, eigen_out, eigen_in, damping):
    bits = devices.bit_length() - 1
    me = lax.axis_index("dp").astype(jnp.int32)
    mine = [(me >> b) & 1 for b in range(bits)]
    per_device = block_pairs.shape[0]
    share = query_gradients.shape[0] // devices
    hot_total = devices // 8

    def across(x, b):
        return lax.ppermute(x, "dp", [(d, d ^ (1 << b)) for d in range(devices)])

    def to_all(x):
        return lax.all_to_all(x, "dp", split_axis=0, concat_axis=0, tiled=True)

    pairs = block_pairs
    for b in range(bits):
        other = across(pairs, b)
        pairs = jnp.where(mine[b] == 0, jnp.concatenate([pairs, other]), jnp.concatenate([other, pairs]))

    rows, hots, first, keep, send = plan(me, pairs, query_gradients, devices, share, hot_total)
    first_share = to_all(first.reshape(devices, share, COLS))
    def halves(x, b, left):
        axis = 1 + sorted(left, reverse=True).index(b)
        left.remove(b)
        keep = lax.dynamic_index_in_dim(x, mine[b], axis, False)
        return keep, lax.dynamic_index_in_dim(x, 1 - mine[b], axis, False)

    def arrived(hot, b, keep, other):
        return jnp.where(((me ^ hot) >> b) & 1 == 1, other, keep)

    inverse = 1.0 / (eigen_out[None, :, None] * eigen_in.reshape(TILES, GROUPED).T[:, None, :] + damping[0])
    other = across(send, 0)
    keep, other = (x.reshape((EXTRA,) + (2,) * (bits - 1) + (share, COLS)) for x in (keep, other))
    chains = []
    for rank in range(hot_total):
        rest = list(range(1, bits))
        turn = rank % 2
        steps = rest[turn : turn + 1] + rest[:turn] + rest[turn + 1 :]
        chains.append([keep, other, 0, steps, rest])

    for k in range(bits - 1):
        if k in (0,):
            sources, plan_of = [], []
            for keep, other, bit, steps, left in chains:
                before = EXTRA * 2 ** sorted(left, reverse=True).index(steps[k])
                sources += [x.reshape(before, 2, -1, COLS) for x in (keep, other)]
                plan_of.append((bit, steps[k]))
                left.remove(steps[k])
            halved = pick(me, hots, sources, tuple(plan_of))
            parts = [
                [x.reshape((EXTRA,) + (2,) * len(chain[4]) + (share, COLS)) for x in halved[2 * r : 2 * r + 2]]
                for r, chain in enumerate(chains)
            ]
        else:
            parts = []
            for rank, (keep, other, bit, steps, left) in enumerate(chains):
                parts.append(halves(arrived(hots[rank], bit, keep, other), steps[k], left))
        sends = [part[1] for part in parts]
        if k == 0:
            *sends, inverse = lax.optimization_barrier((*sends, inverse))
            conditioned = precondition(train_features, basis_in, basis_out, inverse.reshape(WIDE, TILES), devices)
            conditioned, first_share = lax.optimization_barrier((conditioned, first_share))
            train_share = to_all(conditioned)
        if k == bits - 2:
            *sends, train_share = lax.optimization_barrier((*sends, train_share))
        others = [across(send, chain[3][k]) for send, chain in zip(sends, chains)]
        others = lax.optimization_barrier(others)
        for rank, chain in enumerate(chains):
            chain[:3] = parts[rank][0], others[rank], chain[3][k]
    extra_share = jnp.concatenate([arrived(hots[r], chain[2], chain[0], chain[1]) for r, chain in enumerate(chains)])

    keep, send = partial_scores(per_device, me, rows, train_share, first_share, extra_share)
    tiles = (keep + across(send, 0)).reshape((2,) * (bits - 1) + (per_device, COLS, COLS))

    sums, middle = [], list(range(1, bits - 1))
    for pair in range(per_device):
        x, left = tiles[..., pair, :, :], list(range(1, bits))
        turn = pair % 2
        for k, b in enumerate(middle[turn:] + middle[:turn]):
            axis = sorted(left, reverse=True).index(b)
            left.remove(b)
            keep = lax.dynamic_index_in_dim(x, mine[b], axis, False)
            send = lax.dynamic_index_in_dim(x, 1 - mine[b], axis, False)
            if k == 0:
                x = keep + across(send.astype(bf16), b).astype(f32)
            else:
                x = keep + across(send, b)
        sums.append(x)
    tiles = jnp.stack(sums, axis=1)
    keep = lax.dynamic_index_in_dim(tiles, mine[-1], 0, False)
    send = lax.dynamic_index_in_dim(tiles, 1 - mine[-1], 0, False)
    tiles = keep + across(send, bits - 1)
    return tiles


def solution(mesh):
    placed = (
        P(None, ("groups", "dp")),
        P(None, ("groups", "dp")),
        P(("groups", "dp"), None),
        P("groups", None),
        P("groups", None),
        P("groups"),
        P("groups"),
        P("groups"),
    )
    return jax.shard_map(
        functools.partial(body, mesh.shape["dp"]),
        mesh=mesh,
        in_specs=placed,
        out_specs=P(("groups", "dp"), None, None),
        check_vma=False,
    )
```
